32 devices in a mesh: dp: 4 (over y, x), expert: 8 (over z, core).
Axes of the slice: x: 2, y: 2, z: 4, core: 2. Of those that a mesh axis runs over, the one named last changes fastest.
Arguments:
- tokens: bfloat16 [4096, 3584], P(('dp', 'expert')), may hold values from -6 to 6
- gate_up: bfloat16 [8, 3584, 2048], P('expert', 'dp'), may hold values from -0.09375 to 0.09375
- down_proj: bfloat16 [8, 1024, 3584], P('expert', None, 'dp'), may hold values from -0.1875 to 0.1875
- expert_ids: int32 [4096, 8], P(('dp', 'expert')), may hold values from 0 to 31, all different within a row; in each aligned block of 128 rows (0 to 127, 128 to 255, ...) at most 64 rows name the same one
- gate_weights: bfloat16 [4096, 8], P(('dp', 'expert')), may hold values from 0.049804688 to 1
Outputs:
- mixed: bfloat16 [4096, 3584], P(('dp', 'expert'))
The draws below stay inside these ranges and needn't reach their ends.
Inputs may be any that keep to these rules, and one draw needn't show every extreme that they name: `expert_ids`: A row names 8 different experts. Among the rows of one device (aligned blocks of 128 rows), no expert is named by more than 64 rows.
All inputs are finite; a program needn't handle non-finite values.
Results may differ from the reference program's by a relative error of at most 0.0058.
Values may be sent and summed in bfloat16 or wider, within the bound.
No kernel may reach another device: no remote copies, remote signals or barrier semaphores. Data moves between devices by JAX's collectives and lax.ppermute only.
A program may use at most 128 MiB of HBM per device.

```python
import math
import jax
import jax.numpy as jnp
import numpy as np
from jax import lax

D = 3584
FF = 1024
TOP = 8
TOK_DEV = 128
EXPERTS = 32
COMPUTED = 8
CAP = 64
TOKENS = 4096
N_DP = 4
N_EXPERT = 8


def shard_levels(stream_key, dims, shards, low, high):
    loudness, own = 1.0, jax.random.fold_in(stream_key, 6)
    for position, shards_of in shards:
        heights = jnp.exp(jax.random.uniform(jax.random.fold_in(own, position), (shards_of,), jnp.float32, low / len(shards), high / len(shards)))
        loudness = loudness * jnp.repeat(heights, dims[position] // shards_of).reshape([-1 if axis == position else 1 for axis in range(len(dims))])
    return loudness


def assign_block(rng, own, number, rows, number_of, top, limit, skew):
    ranking = jax.random.permutation(rng, number_of)
    packed, common = shares(number_of, rows * top, limit, skew, True), shares(number_of, rows * top, limit, skew, False)
    places = jnp.arange(number_of)

    def named(sizes, offset_by):
        used = int((sizes > 0).sum())
        fixed = max(1, used // 4)
        shifted = fixed + (places - fixed + offset_by * (used - fixed)) % max(1, number_of - fixed)
        return jnp.zeros((number_of,), jnp.int32).at[ranking[jnp.where(places < fixed, places, shifted)]].set(jnp.asarray(sizes, jnp.int32))

    sizes = jnp.where(number % 4 == 0, named(packed, number // 4), named(common, number - number // 4 - 1))
    mixed = jax.random.permutation(jax.random.fold_in(own, 3), number_of)
    donor, sink = mixed[0:number_of // 2 * 2:2], mixed[1:number_of // 2 * 2:2]
    margin = jnp.minimum(sizes[donor] - 1, limit - sizes[sink]) // 2
    margin = jnp.where((donor == ranking[0]) | (sink == ranking[0]) | (sizes[sink] == 0), 0, jnp.maximum(margin, 0))
    shifted = jax.random.randint(jax.random.fold_in(own, 4), (number_of // 2,), 0, 1 << 20) % (margin + 1)
    sizes = sizes.at[donor].add(-shifted).at[sink].add(shifted)
    members = jnp.searchsorted(jnp.cumsum(sizes), jnp.arange(rows * top), side="right").astype(jnp.int32)
    grid = members.reshape(top, rows).T
    grid = grid[jax.random.permutation(jax.random.fold_in(own, 1), rows)]
    offset_by = jax.random.randint(jax.random.fold_in(own, 2), (rows, 1), 0, top)
    return jnp.take_along_axis(grid, (jnp.arange(top)[None, :] + offset_by) % top, axis=1)


def shares(count, total, limit, skew, full):
    loads = [(1 << 20) // math.isqrt(standing ** skew) + 1 for standing in range(1, count + 1)]
    largest = limit if full else min(limit, max(-(-total // count), total * loads[0] // sum(loads)))
    least = 1 if total - largest >= count - 1 else 0
    counts, spare = [largest] + [least] * (count - 1), total - largest - least * (count - 1)
    while spare > 0:
        candidates = [i for i in range(1, count) if counts[i] < largest] or [i for i in range(1, count) if counts[i] < limit]
        whole, budget = sum([loads[i] for i in candidates]), spare
        for i in candidates:
            addition = min(limit - counts[i], max(1, budget * loads[i] // whole), spare)
            counts[i] = counts[i] + addition
            spare = spare - addition
    return np.array(counts)


def noise(rng, shape, scale, bound, shards=(), kind=jnp.bfloat16):
    drawn = scale * jax.random.normal(rng, shape, jnp.float32)
    if shards:
        drawn = drawn * shard_levels(rng, shape, shards, -0.22, 0.18)
    return jnp.clip(drawn, -bound, bound).astype(kind)


def setup_inputs(seed: int = 0) -> dict:
    arg_keys = jax.random.split(jax.random.key(seed), 6)
    tokens = noise(arg_keys[0], (TOKENS, D), 1.0, 6.0, ((0, 32),))
    gate_up = noise(arg_keys[1], (COMPUTED, D, 2 * FF), D ** -0.5, 0.09375, ((0, 8), (1, 4)))
    down_proj = noise(arg_keys[2], (COMPUTED, FF, D), FF ** -0.5, 0.1875, ((0, 8), (2, 4)))
    expert_ids_keys = jax.random.split(jax.random.fold_in(arg_keys[3], 1), TOKENS // TOK_DEV)
    expert_ids_turns = jax.random.permutation(jax.random.fold_in(arg_keys[3], 3), TOKENS // TOK_DEV)
    expert_ids = jax.vmap(lambda own, number: assign_block(jax.random.fold_in(arg_keys[3], 2), own, number, TOK_DEV, EXPERTS, TOP, CAP, 1))(expert_ids_keys, expert_ids_turns).reshape((TOKENS, TOP))
    gate_weights = jnp.clip(jnp.exp(math.log(1.0) - 2.9996462 * jax.random.uniform(arg_keys[4], (TOKENS, TOP), jnp.float32) ** shard_levels(arg_keys[4], (TOKENS, TOP), ((0, 32),), -0.2, 0.2)), 0.049804688, 1.0).astype(jnp.bfloat16)
    return dict(tokens=tokens, gate_up=gate_up, down_proj=down_proj, expert_ids=expert_ids, gate_weights=gate_weights)


def reference(tokens, gate_up, down_proj, expert_ids, gate_weights):
    most_rows = N_DP * N_EXPERT * CAP
    positions = jnp.arange(most_rows, dtype=jnp.int32)

    def one_expert(total, expert):
        hits = (expert_ids == expert)
        picked = jnp.any(hits, axis=1)
        count = jnp.sum(picked.astype(jnp.int32))
        index = jnp.nonzero(picked, size=most_rows, fill_value=0)[0].astype(jnp.int32)
        valid = positions < count
        weight = jnp.sum(jnp.where(hits[index], gate_weights[index].astype(jnp.float32), 0.0), axis=1)
        weight = jnp.where(valid, weight, 0.0)
        rows = tokens[index]
        weights_gu = lax.dynamic_index_in_dim(gate_up, expert, 0, keepdims=False)
        weights_down = lax.dynamic_index_in_dim(down_proj, expert, 0, keepdims=False)
        gu = jnp.dot(rows, weights_gu, preferred_element_type=jnp.float32)
        hidden = (jax.nn.silu(gu[:, :FF]) * gu[:, FF:]).astype(jnp.bfloat16)
        output = jnp.dot(hidden, weights_down, preferred_element_type=jnp.float32).astype(jnp.bfloat16)
        total = total.at[index].add(weight[:, None] * output.astype(jnp.float32))
        return total, None

    start = jnp.zeros((TOKENS, D), jnp.float32)
    total, unused = lax.scan(one_expert, start, jnp.arange(COMPUTED, dtype=jnp.int32))
    return total.astype(jnp.bfloat16)
```

```python
import jax
import jax.numpy as jnp
from jax import lax
from jax.sharding import PartitionSpec as P

BF = jnp.bfloat16
F32 = jnp.float32


def gathered(tokens, gate_up, down_proj, expert_ids, gate_weights):
    owners = lax.axis_size("expert")
    tok_rows = tokens.shape[0]
    width = tokens.shape[1]
    hidden_units = down_proj.shape[1]
    slots = 4 * tok_rows // owners
    total_rows = owners * slots
    owner_ids = jnp.arange(owners, dtype=jnp.int32)
    matches = expert_ids[:, :, None] == owner_ids[None, None, :]
    hits = jnp.sum(matches.astype(jnp.int32), axis=1)
    pick_weight = jnp.sum(
        jnp.where(matches, gate_weights[:, :, None].astype(F32), 0.0), axis=1
    )
    before = jnp.cumsum(hits, axis=0) - hits
    target = jnp.where(hits > 0, owner_ids[None, :] * slots + before, -1)
    slot_owner = jnp.arange(total_rows, dtype=jnp.int32) // slots
    slot_ids = jnp.arange(total_rows, dtype=jnp.int32)
    placed = jnp.take(target, slot_owner, axis=1) == slot_ids[None, :]
    place_bf = placed.astype(BF)
    outgoing = jnp.dot(place_bf.T, tokens, preferred_element_type=F32).astype(BF)
    arrived = lax.all_to_all(
        outgoing.reshape(owners, slots, width), "expert", split_axis=0, concat_axis=0, tiled=True
    )
    rows = arrived.reshape(total_rows, width)
    gu = jnp.dot(
        rows,
        lax.all_gather(gate_up, "dp", axis=1, tiled=True)[0],
        preferred_element_type=F32,
    )
    hidden = (jax.nn.silu(gu[:, :hidden_units]) * gu[:, hidden_units:]).astype(BF)
    result = jnp.dot(
        hidden,
        lax.all_gather(down_proj, "dp", axis=2, tiled=True)[0],
        preferred_element_type=F32,
    ).astype(BF)
    returned = lax.all_to_all(
        result.reshape(owners, slots, width), "expert", split_axis=0, concat_axis=0, tiled=True
    )
    weighted = (place_bf.astype(F32) * jnp.take(pick_weight, slot_owner, axis=1)).astype(BF)
    mixed = jnp.dot(weighted, returned.reshape(total_rows, width), preferred_element_type=F32)
    return mixed.astype(BF)


def swap(value, axis, bit):
    return lax.ppermute(value, axis, [(i, i ^ bit) for i in range(lax.axis_size(axis))])


def paired(tokens, gate_up, down_proj, expert_ids, gate_weights):
    owners = lax.axis_size("expert")
    chips = owners // 2
    tok = tokens.shape[0]
    quarter = gate_up.shape[1]
    ff = down_proj.shape[1]
    slots = 4 * tok // owners
    d = lax.axis_index("dp")
    e = lax.axis_index("expert")
    z, core = e // 2, e % 2
    gate, down = gate_up[0], down_proj[0]

    gate_x = swap(gate, "dp", 1)
    parts = [
        lax.dynamic_slice_in_dim(tokens, (d ^ r) * quarter, quarter, axis=1) for r in range(4)
    ]
    theirs = swap(jnp.concatenate(parts[2:], axis=1), "dp", 2)
    both = jnp.stack([jnp.concatenate(parts[:2], axis=1), theirs])
    down_y = swap(down, "dp", 2)

    meta = lax.all_gather(
        jnp.concatenate([expert_ids.astype(BF), gate_weights], axis=1), ("dp", "expert")
    ).reshape(4, chips, 2, tok, -1)
    meta = lax.dynamic_index_in_dim(meta, core, 2, keepdims=False)
    meta = jnp.stack(
        [lax.dynamic_index_in_dim(meta, d ^ r, 0, keepdims=False) for r in range(3)]
    )
    top = expert_ids.shape[1]
    ids = meta[..., :top].astype(jnp.int32)
    chosen = jnp.stack([e, e ^ 1]).astype(jnp.int32)
    matches = ids[..., None] == chosen
    hits = jnp.any(matches, axis=3)
    weight = jnp.sum(jnp.where(matches, meta[..., top:, None].astype(F32), 0.0), axis=3)
    hits = hits.transpose(0, 1, 3, 2)
    weight = weight.transpose(0, 1, 3, 2)
    earlier = jnp.triu(jnp.ones((tok, tok), BF), 1)
    rank = jnp.dot(hits.astype(BF), earlier, preferred_element_type=F32)
    rank = jnp.where(hits, rank, -1.0)
    placed = rank[..., None, :] == jnp.arange(slots, dtype=F32)[:, None]
    place = placed.astype(BF)
    pay = (place * weight[..., None, :].astype(BF))[:2].reshape(2, chips, 2 * slots, tok)

    line = [list(range(c, owners, 2)) for c in range(2)]
    seen = lax.all_gather(both, "expert", axis_index_groups=line)
    sel = place[::2]

    def choose(expert):
        return jnp.einsum(
            "gzst,zgtk->gzsk", sel[:, :, expert], seen, preferred_element_type=F32
        ).astype(BF)

    other = swap(choose(1), "expert", 1)
    rows = jnp.stack([choose(0), other], axis=2).reshape(2 * owners * slots, 2 * quarter)

    part = jnp.dot(rows[:, :quarter], gate, preferred_element_type=F32) + jnp.dot(
        rows[:, quarter:], gate_x, preferred_element_type=F32
    )
    half = owners * slots
    gu = part[:half] + swap(part[half:].astype(BF), "dp", 2).astype(F32)
    hidden = (jax.nn.silu(gu[:, :ff]) * gu[:, ff:]).astype(BF)
    hiddens = [hidden, swap(hidden, "dp", 1)]

    mine = []
    for g in range(2):
        out = jnp.concatenate(
            [jnp.dot(hiddens[g], w, preferred_element_type=F32).astype(BF) for w in (down, down_y)],
            axis=1,
        ).reshape(chips, 2, slots, 2 * quarter)
        back = swap(out[:, 1], "expert", 1)
        out = jnp.concatenate([out[:, 0], back], axis=1)

        def term(chip):
            chip = jnp.clip(chip, 0, chips - 1)
            return lax.dot_general(
                lax.dynamic_index_in_dim(pay[g], chip, 0, keepdims=False),
                lax.dynamic_index_in_dim(out, chip, 0, keepdims=False),
                (((0,), (0,)), ((), ())),
                preferred_element_type=F32,
            )

        up = down_line = 0.0
        for k in range(1, chips):
            up = lax.ppermute(
                (term(z + chips - k) + up).astype(BF),
                "expert",
                [(2 * i + c, 2 * i + 2 + c) for i in range(k) for c in range(2)],
            ).astype(F32)
            down_line = lax.ppermute(
                (term(z - chips + k) + down_line).astype(BF),
                "expert",
                [
                    (2 * i + c, 2 * i - 2 + c)
                    for i in range(chips - k, chips)
                    for c in range(2)
                ],
            ).astype(F32)
        mine.append((term(z) + up + down_line).astype(BF))

    far = swap(mine[1], "dp", 1)
    mixed = jnp.zeros(tokens.shape, BF)
    for r, piece in enumerate(
        [mine[0][:, :quarter], far[:, :quarter], mine[0][:, quarter:], far[:, quarter:]]
    ):
        mixed = lax.dynamic_update_slice_in_dim(mixed, piece, (d ^ r) * quarter, axis=1)
    return mixed


def solution(mesh):
    placed = (
        P(("dp", "expert"), None),
        P("expert", "dp", None),
        P("expert", None, "dp"),
        P(("dp", "expert"), None),
        P(("dp", "expert"), None),
    )
    short = mesh.shape["expert"] <= 8 and mesh.shape["dp"] == 4
    return jax.shard_map(
        paired if short else gathered,
        mesh=mesh,
        in_specs=placed,
        out_specs=P(("dp", "expert"), None),
        check_vma=False,
    )
```

```python
import jax
import jax.numpy as jnp
from jax import lax
from jax.sharding import PartitionSpec as P

BF = jnp.bfloat16
F32 = jnp.float32


def gathered(tokens, gate_up, down_proj, expert_ids, gate_weights):
    owners = lax.axis_size("expert")
    tok_rows = tokens.shape[0]
    width = tokens.shape[1]
    hidden_units = down_proj.shape[1]
    slots = 4 * tok_rows // owners
    total_rows = owners * slots
    owner_ids = jnp.arange(owners, dtype=jnp.int32)
    matches = expert_ids[:, :, None] == owner_ids[None, None, :]
    hits = jnp.sum(matches.astype(jnp.int32), axis=1)
    pick_weight = jnp.sum(
        jnp.where(matches, gate_weights[:, :, None].astype(F32), 0.0), axis=1
    )
    before = jnp.cumsum(hits, axis=0) - hits
    target = jnp.where(hits > 0, owner_ids[None, :] * slots + before, -1)
    slot_owner = jnp.arange(total_rows, dtype=jnp.int32) // slots
    slot_ids = jnp.arange(total_rows, dtype=jnp.int32)
    placed = jnp.take(target, slot_owner, axis=1) == slot_ids[None, :]
    place_bf = placed.astype(BF)
    outgoing = jnp.dot(place_bf.T, tokens, preferred_element_type=F32).astype(BF)
    arrived = lax.all_to_all(
        outgoing.reshape(owners, slots, width), "expert", split_axis=0, concat_axis=0, tiled=True
    )
    rows = arrived.reshape(total_rows, width)
    gu = jnp.dot(
        rows,
        lax.all_gather(gate_up, "dp", axis=1, tiled=True)[0],
        preferred_element_type=F32,
    )
    hidden = (jax.nn.silu(gu[:, :hidden_units]) * gu[:, hidden_units:]).astype(BF)
    result = jnp.dot(
        hidden,
        lax.all_gather(down_proj, "dp", axis=2, tiled=True)[0],
        preferred_element_type=F32,
    ).astype(BF)
    returned = lax.all_to_all(
        result.reshape(owners, slots, width), "expert", split_axis=0, concat_axis=0, tiled=True
    )
    weighted = (place_bf.astype(F32) * jnp.take(pick_weight, slot_owner, axis=1)).astype(BF)
    mixed = jnp.dot(weighted, returned.reshape(total_rows, width), preferred_element_type=F32)
    return mixed.astype(BF)


def swap(value, axis, bit):
    return lax.ppermute(value, axis, [(i, i ^ bit) for i in range(lax.axis_size(axis))])


def order_of(chips):
    def step(chip, to):
        return chips - abs(to - chip) if to != chip else chips

    return [sorted(range(chips), key=lambda to: (step(chip, to), to)) for chip in range(chips)]


def paired(tokens, gate_up, down_proj, expert_ids, gate_weights):
    owners = lax.axis_size("expert")
    chips = owners // 2
    tok = tokens.shape[0]
    top = expert_ids.shape[1]
    quarter = gate_up.shape[1]
    half = 2 * quarter
    ff = down_proj.shape[1]
    slots = 4 * tok // owners
    d = lax.axis_index("dp")
    e = lax.axis_index("expert")
    z = e // 2
    gate, down = gate_up[0], down_proj[0]
    order = jnp.array(order_of(chips), jnp.int32)[z]

    def hop(value, sources, by):
        return lax.ppermute(
            value, "expert", [(2 * i + c, 2 * (i + by) + c) for i in sources for c in range(2)]
        )

    info = jnp.concatenate([expert_ids.astype(BF), gate_weights], axis=1)
    info_x = swap(info, "dp", 1)
    gate_x = swap(gate, "dp", 1)
    parts = [
        lax.dynamic_slice_in_dim(tokens, (d ^ r) * quarter, quarter, axis=1) for r in range(4)
    ]
    first = jnp.concatenate([parts[0], parts[1], info], axis=1)
    second = jnp.concatenate([swap(jnp.concatenate([parts[2], parts[3], info], axis=1), "dp", 2), info_x], axis=1)
    down_y = swap(down, "dp", 2)

    seen = []
    for own in (first, second):
        right = left = own
        rights, lefts = {}, {}
        for k in range(1, chips):
            right = rights[k] = hop(right, range(k - 1, chips - 1), 1)
            left = lefts[k] = hop(left, range(1, chips - k + 1), -1)
        seen.append(
            [own] + [jnp.where(z >= k, rights[k], lefts[chips - k]) for k in range(1, chips)]
        )
    info = jnp.stack(
        [
            jnp.stack([s[:, half : half + 2 * top] for s in seen[0]]),
            jnp.stack([s[:, half + 2 * top :] for s in seen[1]]),
            jnp.stack([s[:, half : half + 2 * top] for s in seen[1]]),
        ]
    )
    seen = jnp.stack([jnp.stack([s[:, :half] for s in seen[g]]) for g in range(2)])
    ids = info[..., :top].astype(jnp.int32)
    chosen = jnp.stack([e, e ^ 1]).astype(jnp.int32)
    matches = ids[..., None] == chosen
    hits = jnp.any(matches, axis=3).transpose(0, 1, 3, 2)
    weight = jnp.sum(jnp.where(matches, info[..., top:, None].astype(F32), 0.0), axis=3)
    weight = weight.transpose(0, 1, 3, 2)
    earlier = jnp.triu(jnp.ones((tok, tok), BF), 1)
    rank = jnp.dot(hits.astype(BF), earlier, preferred_element_type=F32)
    rank = jnp.where(hits, rank, -1.0)
    placed = rank[..., None, :] == jnp.arange(slots, dtype=F32)[:, None]
    place = placed.astype(BF)
    pay = (place * weight[..., None, :].astype(BF))[:2].reshape(2, chips, 2 * slots, tok)

    def choose(expert):
        return jnp.einsum(
            "gzst,gztk->zgsk", place[::2, :, expert], seen, preferred_element_type=F32
        ).astype(BF)

    other = swap(choose(1), "expert", 1)
    rows = jnp.stack([choose(0), other], axis=2)
    rows, down_y = lax.optimization_barrier((rows, down_y))
    chunk = 2 * slots
    near = jnp.dot(
        rows[..., :quarter].reshape(-1, quarter), gate, preferred_element_type=F32
    ).reshape(chips, 2, chunk, 2 * ff)

    def pick(array, q):
        return lax.dynamic_index_in_dim(array, (z - order[q]) % chips, 0, keepdims=False)

    terms = []
    for q in range(chips):
        r = pick(rows, q)[..., quarter:].reshape(2, chunk, quarter)
        n = pick(near, q)
        sent = (jnp.dot(r[1], gate_x, preferred_element_type=F32) + n[1]).astype(BF)
        gu = jnp.dot(r[0], gate_x, preferred_element_type=F32) + n[0]
        gu = gu + swap(sent, "dp", 2).astype(F32)
        hidden = (jax.nn.silu(gu[:, :ff]) * gu[:, ff:]).astype(BF)
        hidden = jnp.concatenate([hidden, swap(hidden, "dp", 1)])
        out = jnp.concatenate(
            [jnp.dot(hidden, w, preferred_element_type=F32).astype(BF) for w in (down, down_y)],
            axis=1,
        ).reshape(2, 2, slots, half)
        back = swap(out[:, 1], "expert", 1)
        out = jnp.concatenate([out[:, 0], back], axis=1)
        paid = lax.dynamic_index_in_dim(pay, (z - order[q]) % chips, 1, keepdims=False)
        terms.append(jnp.einsum("gst,gsk->gtk", paid, out, preferred_element_type=F32))

    def term(step, to):
        total = terms[0]
        for q in range(1, min(step, chips - 1)):
            total = jnp.where(order[q] == to, terms[q], total)
        return total

    right = left = 0.0
    for k in range(1, chips):
        right = hop((term(k, z + chips - k) + right).astype(BF), range(k), 1).astype(F32)
        left = hop((term(k, z - chips + k) + left).astype(BF), range(chips - k, chips), -1).astype(F32)
    mine = (terms[-1] + right + left).astype(BF)

    far = swap(mine[1], "dp", 1)
    mixed = jnp.zeros(tokens.shape, BF)
    for r, piece in enumerate(
        [mine[0, :, :quarter], far[:, :quarter], mine[0, :, quarter:], far[:, quarter:]]
    ):
        mixed = lax.dynamic_update_slice_in_dim(mixed, piece, (d ^ r) * quarter, axis=1)
    return mixed


def solution(mesh):
    placed = (
        P(("dp", "expert"), None),
        P("expert", "dp", None),
        P("expert", None, "dp"),
        P(("dp", "expert"), None),
        P(("dp", "expert"), None),
    )
    short = mesh.shape["expert"] <= 8 and mesh.shape["dp"] == 4
    return jax.shard_map(
        paired if short else gathered,
        mesh=mesh,
        in_specs=placed,
        out_specs=P(("dp", "expert"), None),
        check_vma=False,
    )
```

```python
import jax
import jax.numpy as jnp
from jax import lax
from jax.sharding import PartitionSpec as P

BF = jnp.bfloat16
F32 = jnp.float32
CUTS = ((0, 1), (1, 3), (3, 5), (5, 6), (6, 7))


def gathered(tokens, gate_up, down_proj, expert_ids, gate_weights):
    owners = lax.axis_size("expert")
    tok_rows = tokens.shape[0]
    width = tokens.shape[1]
    hidden_units = down_proj.shape[1]
    slots = 4 * tok_rows // owners
    total_rows = owners * slots
    owner_ids = jnp.arange(owners, dtype=jnp.int32)
    matches = expert_ids[:, :, None] == owner_ids[None, None, :]
    hits = jnp.sum(matches.astype(jnp.int32), axis=1)
    pick_weight = jnp.sum(
        jnp.where(matches, gate_weights[:, :, None].astype(F32), 0.0), axis=1
    )
    before = jnp.cumsum(hits, axis=0) - hits
    target = jnp.where(hits > 0, owner_ids[None, :] * slots + before, -1)
    slot_owner = jnp.arange(total_rows, dtype=jnp.int32) // slots
    slot_ids = jnp.arange(total_rows, dtype=jnp.int32)
    placed = jnp.take(target, slot_owner, axis=1) == slot_ids[None, :]
    place_bf = placed.astype(BF)
    outgoing = jnp.dot(place_bf.T, tokens, preferred_element_type=F32).astype(BF)
    arrived = lax.all_to_all(
        outgoing.reshape(owners, slots, width), "expert", split_axis=0, concat_axis=0, tiled=True
    )
    rows = arrived.reshape(total_rows, width)
    gu = jnp.dot(
        rows,
        lax.all_gather(gate_up, "dp", axis=1, tiled=True)[0],
        preferred_element_type=F32,
    )
    hidden = (jax.nn.silu(gu[:, :hidden_units]) * gu[:, hidden_units:]).astype(BF)
    result = jnp.dot(
        hidden,
        lax.all_gather(down_proj, "dp", axis=2, tiled=True)[0],
        preferred_element_type=F32,
    ).astype(BF)
    returned = lax.all_to_all(
        result.reshape(owners, slots, width), "expert", split_axis=0, concat_axis=0, tiled=True
    )
    weighted = (place_bf.astype(F32) * jnp.take(pick_weight, slot_owner, axis=1)).astype(BF)
    mixed = jnp.dot(weighted, returned.reshape(total_rows, width), preferred_element_type=F32)
    return mixed.astype(BF)


def swap(value, axis, bit):
    return lax.ppermute(value, axis, [(i, i ^ bit) for i in range(lax.axis_size(axis))])


def order_of(chips):
    def step(chip, to):
        return chips - abs(to - chip) if to != chip else chips

    return [sorted(range(chips), key=lambda to: (step(chip, to), to)) for chip in range(chips)]


def paired(tokens, gate_up, down_proj, expert_ids, gate_weights):
    owners = lax.axis_size("expert")
    chips = owners // 2
    tok = tokens.shape[0]
    top = expert_ids.shape[1]
    quarter = gate_up.shape[1]
    half = 2 * quarter
    ff = down_proj.shape[1]
    slots = 4 * tok // owners
    d = lax.axis_index("dp")
    e = lax.axis_index("expert")
    z = e // 2
    gate, down = gate_up[0], down_proj[0]
    order = jnp.array(order_of(chips), jnp.int32)[z]

    def hop(value, sources, by):
        return lax.ppermute(
            value, "expert", [(2 * i + c, 2 * (i + by) + c) for i in sources for c in range(2)]
        )

    together = lax.optimization_barrier
    parts = [
        lax.dynamic_slice_in_dim(tokens, (d ^ r) * quarter, quarter, axis=1) for r in range(4)
    ]
    info = jnp.concatenate([expert_ids.astype(BF), gate_weights], axis=1)
    first = jnp.concatenate([parts[0], parts[1], info], axis=1)
    gates = [gate[quarter * lo // 7 : quarter * hi // 7] for lo, hi in CUTS]
    downs = jnp.split(down, 2)

    rights, lefts, down_y, gate_x = [{}, {}], [{}, {}], [], []
    own = [first, None]
    for step in range(chips):
        work = {"gate": swap(gates[step], "dp", 1)}
        if step == 0:
            work["info"] = swap(info, "dp", 1)
            work["pair"] = swap(jnp.concatenate([parts[2], parts[3], info], axis=1), "dp", 2)
        elif step <= 2:
            work["down"] = swap(downs[step - 1], "dp", 2)
        for g in range(2):
            k = step + 1 - g
            if 1 <= k < chips:
                source = own[g]
                work[f"right{g}"] = hop(
                    source if k == 1 else rights[g][k - 1], range(k - 1, chips - 1), 1
                )
                work[f"left{g}"] = hop(
                    source if k == 1 else lefts[g][k - 1], range(1, chips - k + 1), -1
                )
        work = together(work)
        gate_x.append(work["gate"])
        if step == 0:
            own[1] = jnp.concatenate([work["pair"], work["info"]], axis=1)
        elif step <= 2:
            down_y.append(work["down"])
        for g in range(2):
            k = step + 1 - g
            if 1 <= k < chips:
                rights[g][k], lefts[g][k] = work[f"right{g}"], work[f"left{g}"]
    gate_last = swap(gates[-1], "dp", 1)
    down_y = jnp.concatenate(down_y)

    seen = [
        [own[g]] + [jnp.where(z >= k, rights[g][k], lefts[g][chips - k]) for k in range(1, chips)]
        for g in range(2)
    ]
    chosen = jnp.stack([e, e ^ 1]).astype(jnp.int32)
    earlier = jnp.triu(jnp.ones((tok, tok), BF), 1)

    def places(group, at):
        info = jnp.stack([s[:, at : at + 2 * top] for s in seen[group]])
        matches = info[..., :top].astype(jnp.int32)[..., None] == chosen
        hits = jnp.any(matches, axis=2).transpose(0, 2, 1)
        weight = jnp.sum(jnp.where(matches, info[..., top:, None].astype(F32), 0.0), axis=2)
        rank = jnp.dot(hits.astype(BF), earlier, preferred_element_type=F32)
        rank = jnp.where(hits, rank, -1.0)
        place = (rank[..., None, :] == jnp.arange(slots, dtype=F32)[:, None]).astype(BF)
        pay = place * weight.transpose(0, 2, 1)[..., None, :].astype(BF)
        return place, pay.reshape(chips, 2 * slots, tok)

    chunk = 2 * slots
    rows, near, pays = [], [], []
    gate_early = jnp.concatenate(gate_x)
    early = quarter + gate_early.shape[0]
    for g in range(2):
        place, pay = places(g, half)
        pays.append(pay)
        held = jnp.stack([s[:, :half] for s in seen[g]])

        def choose(expert):
            return jnp.einsum(
                "zst,ztk->zsk", place[:, expert], held, preferred_element_type=F32
            ).astype(BF)

        other = swap(choose(1), "expert", 1)
        r = jnp.concatenate([choose(0), other], axis=1)
        flat = r.reshape(-1, half)
        n = jnp.dot(flat[:, :quarter], gate, preferred_element_type=F32) + jnp.dot(
            flat[:, quarter:early], gate_early, preferred_element_type=F32
        )
        rows.append(r[..., early:])
        near.append(n.reshape(chips, chunk, 2 * ff))
    pay = jnp.stack([pays[0], places(1, half + 2 * top)[1]])
    rows, near, pay, gate_last, down_y = together((rows, near, pay, gate_last, down_y))

    def product(g, q):
        at = (z - order[q]) % chips
        r = lax.dynamic_index_in_dim(rows[g], at, 0, keepdims=False)
        return jnp.dot(r, gate_last, preferred_element_type=F32) + lax.dynamic_index_in_dim(
            near[g], at, 0, keepdims=False
        )

    def term(step, to):
        total = terms[0]
        for q in range(1, min(step, chips - 1)):
            total = jnp.where(order[q] == to, terms[q], total)
        return total

    right = left = 0.0
    terms, arrived, hidden, joined = [], None, None, None
    sent = product(1, 0).astype(BF)
    for step in range(chips + 2):
        k = step - 2
        work = {}
        if step < chips:
            work["part"] = swap(sent, "dp", 2)
        if step + 1 < chips:
            work["sent"] = product(1, step + 1).astype(BF)
        if arrived is not None:
            gu = product(0, step - 1) + arrived.astype(F32)
            hidden = (jax.nn.silu(gu[:, :ff]) * gu[:, ff:]).astype(BF)
            work["hidden"] = jnp.concatenate([hidden, swap(hidden, "dp", 1)])
        if joined is not None:
            out = jnp.concatenate(
                [
                    jnp.dot(joined, w, preferred_element_type=F32).astype(BF)
                    for w in (down, down_y)
                ],
                axis=1,
            ).reshape(2, 2, slots, half)
            out = jnp.concatenate([out[:, 0], swap(out[:, 1], "expert", 1)], axis=1)
            paid = lax.dynamic_index_in_dim(pay, (z - order[k]) % chips, 1, keepdims=False)
            work["term"] = jnp.einsum("gst,gsk->gtk", paid, out, preferred_element_type=F32)
        if 1 <= k < chips - 1:
            work["right"] = hop((term(k, z + chips - k) + right).astype(BF), range(k), 1)
            work["left"] = hop(
                (term(k, z - chips + k) + left).astype(BF), range(chips - k, chips), -1
            )
        work = together(work)
        sent, arrived, joined = work.get("sent"), work.get("part"), work.get("hidden")
        if "term" in work:
            terms.append(work["term"])
        if "right" in work:
            right, left = work["right"].astype(F32), work["left"].astype(F32)

    k = chips - 1
    mine = []
    upward = (term(k, z + chips - k) + right).astype(BF)
    downward = (term(k, z - chips + k) + left).astype(BF)
    for g in (1, 0):
        came = [hop(upward[g], range(k), 1), hop(downward[g], range(1, chips), -1)]
        if g == 1:
            came, upward, downward = together((came, upward, downward))
        mine.append((terms[-1][g] + came[0].astype(F32) + came[1].astype(F32)).astype(BF))

    far = swap(mine[0], "dp", 1)
    mixed = jnp.zeros(tokens.shape, BF)
    for r, piece in enumerate(
        [mine[1][:, :quarter], far[:, :quarter], mine[1][:, quarter:], far[:, quarter:]]
    ):
        mixed = lax.dynamic_update_slice_in_dim(mixed, piece, (d ^ r) * quarter, axis=1)
    return mixed


def solution(mesh):
    placed = (
        P(("dp", "expert"), None),
        P("expert", "dp", None),
        P("expert", None, "dp"),
        P(("dp", "expert"), None),
        P(("dp", "expert"), None),
    )
    short = mesh.shape["expert"] <= 8 and mesh.shape["dp"] == 4
    return jax.shard_map(
        paired if short else gathered,
        mesh=mesh,
        in_specs=placed,
        out_specs=P(("dp", "expert"), None),
        check_vma=False,
    )
```

```python
import jax
import jax.numpy as jnp
from jax import lax
from jax.sharding import PartitionSpec as P

BF = jnp.bfloat16
F32 = jnp.float32
CUTS = ((0, 1), (1, 3), (3, 5), (5, 6), (6, 7))


def gathered(tokens, gate_up, down_proj, expert_ids, gate_weights):
    owners = lax.axis_size("expert")
    tok_rows = tokens.shape[0]
    width = tokens.shape[1]
    hidden_units = down_proj.shape[1]
    slots = 4 * tok_rows // owners
    total_rows = owners * slots
    owner_ids = jnp.arange(owners, dtype=jnp.int32)
    matches = expert_ids[:, :, None] == owner_ids[None, None, :]
    hits = jnp.sum(matches.astype(jnp.int32), axis=1)
    pick_weight = jnp.sum(
        jnp.where(matches, gate_weights[:, :, None].astype(F32), 0.0), axis=1
    )
    before = jnp.cumsum(hits, axis=0) - hits
    target = jnp.where(hits > 0, owner_ids[None, :] * slots + before, -1)
    slot_owner = jnp.arange(total_rows, dtype=jnp.int32) // slots
    slot_ids = jnp.arange(total_rows, dtype=jnp.int32)
    placed = jnp.take(target, slot_owner, axis=1) == slot_ids[None, :]
    place_bf = placed.astype(BF)
    outgoing = jnp.dot(place_bf.T, tokens, preferred_element_type=F32).astype(BF)
    arrived = lax.all_to_all(
        outgoing.reshape(owners, slots, width), "expert", split_axis=0, concat_axis=0, tiled=True
    )
    rows = arrived.reshape(total_rows, width)
    gu = jnp.dot(
        rows,
        lax.all_gather(gate_up, "dp", axis=1, tiled=True)[0],
        preferred_element_type=F32,
    )
    hidden = (jax.nn.silu(gu[:, :hidden_units]) * gu[:, hidden_units:]).astype(BF)
    result = jnp.dot(
        hidden,
        lax.all_gather(down_proj, "dp", axis=2, tiled=True)[0],
        preferred_element_type=F32,
    ).astype(BF)
    returned = lax.all_to_all(
        result.reshape(owners, slots, width), "expert", split_axis=0, concat_axis=0, tiled=True
    )
    weighted = (place_bf.astype(F32) * jnp.take(pick_weight, slot_owner, axis=1)).astype(BF)
    mixed = jnp.dot(weighted, returned.reshape(total_rows, width), preferred_element_type=F32)
    return mixed.astype(BF)


def swap(value, axis, bit):
    return lax.ppermute(value, axis, [(i, i ^ bit) for i in range(lax.axis_size(axis))])


def order_of(chips):
    def step(chip, to):
        return chips - abs(to - chip) if to != chip else chips

    return [sorted(range(chips), key=lambda to: (step(chip, to), to)) for chip in range(chips)]


def paired(tokens, gate_up, down_proj, expert_ids, gate_weights):
    owners = lax.axis_size("expert")
    chips = owners // 2
    tok = tokens.shape[0]
    top = expert_ids.shape[1]
    quarter = gate_up.shape[1]
    half = 2 * quarter
    ff = down_proj.shape[1]
    slots = 4 * tok // owners
    d = lax.axis_index("dp")
    e = lax.axis_index("expert")
    z = e // 2
    gate, down = gate_up[0], down_proj[0]
    order = jnp.array(order_of(chips), jnp.int32)[z]

    def hop(value, sources, by):
        return lax.ppermute(
            value, "expert", [(2 * i + c, 2 * (i + by) + c) for i in sources for c in range(2)]
        )

    together = lax.optimization_barrier

    def depths(r):
        return lax.dynamic_slice_in_dim(tokens, (d ^ r) * quarter, quarter, axis=1)

    info = jnp.concatenate([expert_ids.astype(BF), gate_weights], axis=1)
    pair = jnp.concatenate([depths(2), depths(3), info], axis=1)
    pair, tokens, info, gate, down = together((pair, tokens, info, gate, down))
    first = jnp.concatenate([depths(0), depths(1), info], axis=1)

    def piece(step):
        lo, hi = CUTS[step]
        return gate[quarter * lo // 7 : quarter * hi // 7]

    rights, lefts, down_y, gate_x = [{}, {}], [{}, {}], [], []
    own = [first, None]
    ahead = {"gate": piece(0)}
    for step in range(chips):
        work = {"gate": swap(ahead["gate"], "dp", 1)}
        if step == 0:
            work["info"] = swap(info, "dp", 1)
            work["pair"] = swap(pair, "dp", 2)
        elif step <= 2:
            work["down"] = swap(ahead["down"], "dp", 2)
        for g in range(2):
            k = step + 1 - g
            if 1 <= k < chips:
                source = own[g]
                work[f"right{g}"] = hop(
                    source if k == 1 else rights[g][k - 1], range(k - 1, chips - 1), 1
                )
                work[f"left{g}"] = hop(
                    source if k == 1 else lefts[g][k - 1], range(1, chips - k + 1), -1
                )
        later = {"gate": piece(step + 1)}
        if step < 2:
            later["down"] = jnp.split(down, 2)[step]
        work, ahead, gate, down = together((work, later, gate, down))
        gate_x.append(work["gate"])
        if step == 0:
            own[1] = jnp.concatenate([work["pair"], work["info"]], axis=1)
        elif step <= 2:
            down_y.append(work["down"])
        for g in range(2):
            k = step + 1 - g
            if 1 <= k < chips:
                rights[g][k], lefts[g][k] = work[f"right{g}"], work[f"left{g}"]
    gate_last = swap(ahead["gate"], "dp", 1)
    down_y = jnp.concatenate(down_y)

    seen = [
        [own[g]] + [jnp.where(z >= k, rights[g][k], lefts[g][chips - k]) for k in range(1, chips)]
        for g in range(2)
    ]
    chosen = jnp.stack([e, e ^ 1]).astype(jnp.int32)
    earlier = jnp.triu(jnp.ones((tok, tok), BF), 1)

    def places(group, at):
        info = jnp.stack([s[:, at : at + 2 * top] for s in seen[group]])
        matches = info[..., :top].astype(jnp.int32)[..., None] == chosen
        hits = jnp.any(matches, axis=2).transpose(0, 2, 1)
        weight = jnp.sum(jnp.where(matches, info[..., top:, None].astype(F32), 0.0), axis=2)
        rank = jnp.dot(hits.astype(BF), earlier, preferred_element_type=F32)
        rank = jnp.where(hits, rank, -1.0)
        place = (rank[..., None, :] == jnp.arange(slots, dtype=F32)[:, None]).astype(BF)
        pay = place * weight.transpose(0, 2, 1)[..., None, :].astype(BF)
        return place, pay.reshape(chips, 2 * slots, tok)

    chunk = 2 * slots
    helds = [jnp.stack([s[:, :half] for s in seen[g]]) for g in range(2)]
    (place0, pay0), (place1, _), (_, pay1) = (
        places(0, half), places(1, half), places(1, half + 2 * top)
    )
    pay = jnp.stack([pay0, pay1])

    def choose(place, held):
        def of(expert):
            return jnp.einsum(
                "zst,ztk->zsk", place[:, expert], held, preferred_element_type=F32
            ).astype(BF)

        other = swap(of(1), "expert", 1)
        return jnp.concatenate([of(0), other], axis=1).reshape(-1, half)

    place1, gate_last = together((place1, gate_last))
    rows = {1: choose(place1, helds[1])}
    weights = jnp.concatenate([gate, *gate_x, gate_last])

    def pick(array, q, axis=0):
        return lax.dynamic_index_in_dim(array, (z - order[q]) % chips, axis, keepdims=False)

    def product(g):
        return jnp.dot(rows[g], weights, preferred_element_type=F32).reshape(chips, chunk, 2 * ff)

    sent = product(1).astype(BF)
    token = sent

    def in_order(*values):
        return together((values, token))[0]

    part = []
    for q in range(chips):
        (sent,) = in_order(sent)
        token = pick(sent, q)
        part.append(swap(token, "dp", 2))
    place0, held0, weights, pay, down_y = in_order(place0, helds[0], weights, pay, down_y)
    rows[0] = choose(place0, held0)
    near = token = product(0)

    hidden, back, out, terms = {}, {}, {}, []

    def finish(q):
        (came,) = in_order(part[q])
        gu = pick(near, q) + came.astype(F32)
        own = (jax.nn.silu(gu[:, :ff]) * gu[:, ff:]).astype(BF)
        hidden[q] = (own, swap(own, "dp", 1))
        return own

    def down_product(q):
        own, theirs = in_order(*hidden[q])
        if q + 1 < chips:
            own, part[q + 1] = together((own, part[q + 1]))
        joined = jnp.concatenate([own, theirs])
        value = jnp.concatenate(
            [jnp.dot(joined, w, preferred_element_type=F32).astype(BF) for w in (down, down_y)],
            axis=1,
        ).reshape(2, 2, slots, half)
        out[q], away = value[:, 0], value[:, 1]
        back[q] = swap(away, "expert", 1)
        return away

    def weigh(q):
        own, theirs = in_order(out[q], back[q])
        terms.append(
            jnp.einsum(
                "gst,gsk->gtk",
                pick(pay, q, 1),
                jnp.concatenate([own, theirs], axis=1),
                preferred_element_type=F32,
            )
        )
        return terms[-1]

    def term(step, to):
        total = terms[0]
        for q in range(1, min(step, chips - 1)):
            total = jnp.where(order[q] == to, terms[q], total)
        return total

    right = left = None

    def chain(k):
        upward, downward = term(k, z + chips - k), term(k, z - chips + k)
        if right is not None:
            r, l = in_order(right, left)
            upward, downward = upward + r.astype(F32), downward + l.astype(F32)
        return upward.astype(BF), downward.astype(BF)

    for q in range(chips):
        if q == 0:
            token = finish(0)
        if q == 2:
            (right, left), token = together(((right, left), token))
        token = down_product(q)
        if q + 1 < chips:
            token = finish(q + 1)
        token = weigh(q)
        k = q if q >= 2 else 1 - q
        if 1 <= k < chips - 1:
            token = upward, downward = chain(k)
            right = hop(upward, range(k), 1)
            left = hop(downward, range(chips - k, chips), -1)

    k = chips - 1
    mine = []
    upward, downward = chain(k)
    for g in (1, 0):
        came = [hop(upward[g], range(k), 1), hop(downward[g], range(1, chips), -1)]
        if g == 1:
            came, upward, downward = together((came, upward, downward))
        mine.append((terms[-1][g] + came[0].astype(F32) + came[1].astype(F32)).astype(BF))

    far = swap(mine[0], "dp", 1)
    mixed = jnp.zeros(tokens.shape, BF)
    for r, piece in enumerate(
        [mine[1][:, :quarter], far[:, :quarter], mine[1][:, quarter:], far[:, quarter:]]
    ):
        mixed = lax.dynamic_update_slice_in_dim(mixed, piece, (d ^ r) * quarter, axis=1)
    return mixed


def solution(mesh):
    placed = (
        P(("dp", "expert"), None),
        P("expert", "dp", None),
        P("expert", None, "dp"),
        P(("dp", "expert"), None),
        P(("dp", "expert"), None),
    )
    short = mesh.shape["expert"] <= 8 and mesh.shape["dp"] == 4
    return jax.shard_map(
        paired if short else gathered,
        mesh=mesh,
        in_specs=placed,
        out_specs=P(("dp", "expert"), None),
        check_vma=False,
    )
```

```python
import jax
import jax.numpy as jnp
from jax import lax
from jax.sharding import PartitionSpec as P

BF = jnp.bfloat16
F32 = jnp.float32
CUTS = ((0, 3), (3, 6), (6, 7))


def gathered(tokens, gate_up, down_proj, expert_ids, gate_weights):
    owners = lax.axis_size("expert")
    tok_rows = tokens.shape[0]
    width = tokens.shape[1]
    hidden_units = down_proj.shape[1]
    slots = 4 * tok_rows // owners
    total_rows = owners * slots
    owner_ids = jnp.arange(owners, dtype=jnp.int32)
    matches = expert_ids[:, :, None] == owner_ids[None, None, :]
    hits = jnp.sum(matches.astype(jnp.int32), axis=1)
    pick_weight = jnp.sum(
        jnp.where(matches, gate_weights[:, :, None].astype(F32), 0.0), axis=1
    )
    before = jnp.cumsum(hits, axis=0) - hits
    target = jnp.where(hits > 0, owner_ids[None, :] * slots + before, -1)
    slot_owner = jnp.arange(total_rows, dtype=jnp.int32) // slots
    slot_ids = jnp.arange(total_rows, dtype=jnp.int32)
    placed = jnp.take(target, slot_owner, axis=1) == slot_ids[None, :]
    place_bf = placed.astype(BF)
    outgoing = jnp.dot(place_bf.T, tokens, preferred_element_type=F32).astype(BF)
    arrived = lax.all_to_all(
        outgoing.reshape(owners, slots, width), "expert", split_axis=0, concat_axis=0, tiled=True
    )
    rows = arrived.reshape(total_rows, width)
    gu = jnp.dot(
        rows,
        lax.all_gather(gate_up, "dp", axis=1, tiled=True)[0],
        preferred_element_type=F32,
    )
    hidden = (jax.nn.silu(gu[:, :hidden_units]) * gu[:, hidden_units:]).astype(BF)
    result = jnp.dot(
        hidden,
        lax.all_gather(down_proj, "dp", axis=2, tiled=True)[0],
        preferred_element_type=F32,
    ).astype(BF)
    returned = lax.all_to_all(
        result.reshape(owners, slots, width), "expert", split_axis=0, concat_axis=0, tiled=True
    )
    weighted = (place_bf.astype(F32) * jnp.take(pick_weight, slot_owner, axis=1)).astype(BF)
    mixed = jnp.dot(weighted, returned.reshape(total_rows, width), preferred_element_type=F32)
    return mixed.astype(BF)


def paired(tokens, gate_up, down_proj, expert_ids, gate_weights):
    owners = lax.axis_size("expert")
    chips = owners // 2
    tok = tokens.shape[0]
    top = expert_ids.shape[1]
    quarter = gate_up.shape[1]
    half = 2 * quarter
    ff = down_proj.shape[1]
    slots = 4 * tok // owners
    chunk = 2 * slots
    d = lax.axis_index("dp")
    e = lax.axis_index("expert")
    gate, down = gate_up[0], down_proj[0]
    together = lax.optimization_barrier

    def send(value, along=0, flip=0, core=0):
        return lax.ppermute(
            value,
            ("dp", "expert"),
            [
                (i * owners + j, (i ^ flip) * owners + ((j ^ core) + 2 * along) % owners)
                for i in range(4)
                for j in range(owners)
            ],
        )

    def depths(r):
        return lax.dynamic_slice_in_dim(tokens, (d ^ r) * quarter, quarter, axis=1)

    info = jnp.concatenate([expert_ids.astype(BF), gate_weights], axis=1)
    first = jnp.concatenate([depths(0), depths(1), info], axis=1)
    second = jnp.concatenate([depths(2), depths(3), info], axis=1)
    gate_x = [
        send(gate[quarter * lo // 7 : quarter * hi // 7], flip=1) for lo, hi in CUTS
    ]
    down_y = send(down, flip=2)

    seen = [{0: first, 1: send(first, 1)}, {1: send(second, 1, 2), 0: send(second, 0, 2)}]
    seen[0][3], seen[1][3] = send(first, -1), send(second, -1, 2)
    seen[0][1], seen[1][1], gate_x[0] = together((seen[0][1], seen[1][1], gate_x[0]))
    seen[0][2], seen[1][2] = send(seen[0][1], 1), send(seen[1][1], 1)
    seen, gate_x[1], down_y = together((seen, gate_x[1], down_y))

    chosen = jnp.stack([e, e ^ 1]).astype(jnp.int32)
    earlier = jnp.triu(jnp.ones((tok, tok), BF), 1)

    def places(info):
        matches = info[..., :top].astype(jnp.int32)[..., None] == chosen
        hits = jnp.any(matches, axis=2).transpose(0, 2, 1)
        weight = jnp.sum(jnp.where(matches, info[..., top:, None].astype(F32), 0.0), axis=2)
        rank = jnp.dot(hits.astype(BF), earlier, preferred_element_type=F32)
        rank = jnp.where(hits, rank, -1.0)
        place = (rank[..., None, :] == jnp.arange(slots, dtype=F32)[:, None]).astype(BF)
        pay = place * weight.transpose(0, 2, 1)[..., None, :].astype(BF)
        return place, pay.reshape(chips, chunk, tok)

    infos = [jnp.stack([seen[g][k][:, half:] for k in range(chips)]) for g in range(2)]
    helds = [jnp.stack([seen[g][k][:, :half] for k in range(chips)]) for g in range(2)]
    info_x = send(infos[0], flip=1)
    place0, pay0 = places(infos[0])
    place1, _ = places(infos[1])
    place1, gate_x[2] = together((place1, gate_x[2]))

    def choose(place, held):
        def of(expert):
            return jnp.einsum(
                "zst,ztk->zsk", place[:, expert], held, preferred_element_type=F32
            ).astype(BF)

        other = send(of(1), core=1)
        return jnp.concatenate([of(0), other], axis=1).reshape(-1, half)

    weights = jnp.concatenate([gate, *gate_x])

    def product(rows):
        return jnp.dot(rows, weights, preferred_element_type=F32).reshape(chips, chunk, 2 * ff)

    order = (2, 1, 3, 0)
    sent = product(choose(place1, helds[1])).astype(BF)
    sent, place0 = together((sent, place0))
    part = [send(sent[k], flip=2) for k in order]
    near = product(choose(place0, helds[0]))
    pay = jnp.stack([pay0, places(info_x)[1]])

    hidden, away, out = {}, {}, {}

    def finish(q, came):
        gu = near[order[q]] + came.astype(F32)
        own = (jax.nn.silu(gu[:, :ff]) * gu[:, ff:]).astype(BF)
        hidden[q] = (own, send(own, flip=1))

    def down_product(q):
        own = hidden[q][0]
        if q + 1 < chips:
            own, part[q + 1] = together((own, part[q + 1]))
        joined = jnp.concatenate([own, hidden[q][1]])
        value = jnp.concatenate(
            [jnp.dot(joined, w, preferred_element_type=F32).astype(BF) for w in (down, down_y)],
            axis=1,
        ).reshape(2, 2, slots, half)
        out[q], away[q] = value[:, 0], value[:, 1]

    def weigh(q, came):
        rows = jnp.concatenate([out[q], came], axis=1)
        return jnp.einsum("gst,gsk->gtk", pay[:, order[q]], rows, preferred_element_type=F32)

    def before_down(q, value):
        own, value = together((hidden[q][0], value))
        hidden[q] = (own, hidden[q][1])
        return value

    finish(0, part[0])
    down_product(0)
    away[0], part[1] = together((away[0], part[1]))
    finish(1, part[1])
    term = before_down(1, weigh(0, send(away[0], core=1)).astype(BF))
    middle = send(term, 1)
    down_product(1)
    away[1], part[2] = together((away[1], part[2]))
    finish(2, part[2])
    term = weigh(1, before_down(2, send(away[1], core=1))).astype(BF)
    back = [send(term[0], -1), send(term[1], -1, 1)]
    middle = before_down(2, middle)
    down_product(2)
    away[2], part[3] = together((away[2], part[3]))
    finish(3, part[3])
    term = (weigh(2, before_down(3, send(away[2], core=1))) + middle.astype(F32)).astype(BF)
    forth = [send(term[0], 1), send(term[1], 1, 1)]
    back[0] = before_down(3, back[0])
    down_product(3)
    term = weigh(3, send(away[3], core=1))
    theirs = send(term[1].astype(BF), flip=1)
    mine = (term[0] + back[0].astype(F32) + forth[0].astype(F32)).astype(BF)
    far = (theirs.astype(F32) + back[1].astype(F32) + forth[1].astype(F32)).astype(BF)

    mixed = jnp.zeros(tokens.shape, BF)
    for r, piece in enumerate(
        [mine[:, :quarter], far[:, :quarter], mine[:, quarter:], far[:, quarter:]]
    ):
        mixed = lax.dynamic_update_slice_in_dim(mixed, piece, (d ^ r) * quarter, axis=1)
    return mixed


def solution(mesh):
    placed = (
        P(("dp", "expert"), None),
        P("expert", "dp", None),
        P("expert", None, "dp"),
        P(("dp", "expert"), None),
        P(("dp", "expert"), None),
    )
    short = mesh.shape["expert"] == 8 and mesh.shape["dp"] == 4
    return jax.shard_map(
        paired if short else gathered,
        mesh=mesh,
        in_specs=placed,
        out_specs=P(("dp", "expert"), None),
        check_vma=False,
    )
```

```python
import jax
import jax.numpy as jnp
from jax import lax
from jax.sharding import PartitionSpec as P

BF = jnp.bfloat16
F32 = jnp.float32
CUTS = ((0, 3), (3, 6), (6, 7))


def gathered(tokens, gate_up, down_proj, expert_ids, gate_weights):
    owners = lax.axis_size("expert")
    tok_rows = tokens.shape[0]
    width = tokens.shape[1]
    hidden_units = down_proj.shape[1]
    slots = 4 * tok_rows // owners
    total_rows = owners * slots
    owner_ids = jnp.arange(owners, dtype=jnp.int32)
    matches = expert_ids[:, :, None] == owner_ids[None, None, :]
    hits = jnp.sum(matches.astype(jnp.int32), axis=1)
    pick_weight = jnp.sum(
        jnp.where(matches, gate_weights[:, :, None].astype(F32), 0.0), axis=1
    )
    before = jnp.cumsum(hits, axis=0) - hits
    target = jnp.where(hits > 0, owner_ids[None, :] * slots + before, -1)
    slot_owner = jnp.arange(total_rows, dtype=jnp.int32) // slots
    slot_ids = jnp.arange(total_rows, dtype=jnp.int32)
    placed = jnp.take(target, slot_owner, axis=1) == slot_ids[None, :]
    place_bf = placed.astype(BF)
    outgoing = jnp.dot(place_bf.T, tokens, preferred_element_type=F32).astype(BF)
    arrived = lax.all_to_all(
        outgoing.reshape(owners, slots, width), "expert", split_axis=0, concat_axis=0, tiled=True
    )
    rows = arrived.reshape(total_rows, width)
    gu = jnp.dot(
        rows,
        lax.all_gather(gate_up, "dp", axis=1, tiled=True)[0],
        preferred_element_type=F32,
    )
    hidden = (jax.nn.silu(gu[:, :hidden_units]) * gu[:, hidden_units:]).astype(BF)
    result = jnp.dot(
        hidden,
        lax.all_gather(down_proj, "dp", axis=2, tiled=True)[0],
        preferred_element_type=F32,
    ).astype(BF)
    returned = lax.all_to_all(
        result.reshape(owners, slots, width), "expert", split_axis=0, concat_axis=0, tiled=True
    )
    weighted = (place_bf.astype(F32) * jnp.take(pick_weight, slot_owner, axis=1)).astype(BF)
    mixed = jnp.dot(weighted, returned.reshape(total_rows, width), preferred_element_type=F32)
    return mixed.astype(BF)


def paired(tokens, gate_up, down_proj, expert_ids, gate_weights):
    owners = lax.axis_size("expert")
    chips = owners // 2
    tok = tokens.shape[0]
    top = expert_ids.shape[1]
    quarter = gate_up.shape[1]
    half = 2 * quarter
    ff = down_proj.shape[1]
    slots = 4 * tok // owners
    chunk = 2 * slots
    d = lax.axis_index("dp")
    e = lax.axis_index("expert")
    gate, down = gate_up[0], down_proj[0]
    together = lax.optimization_barrier

    def send(value, along=0, flip=0, core=0):
        return lax.ppermute(
            value,
            ("dp", "expert"),
            [
                (i * owners + j, (i ^ flip) * owners + ((j ^ core) + 2 * along) % owners)
                for i in range(4)
                for j in range(owners)
            ],
        )

    def depths(r):
        return lax.dynamic_slice_in_dim(tokens, (d ^ r) * quarter, quarter, axis=1)

    info = jnp.concatenate([expert_ids.astype(BF), gate_weights], axis=1).T
    info = jnp.pad(info, ((0, 0), (0, half - tok)))

    def payload(r):
        return jnp.concatenate([jnp.concatenate([depths(r), depths(r + 1)], axis=1), info])

    first, second = payload(0), payload(2)
    gate_x = [
        send(gate[quarter * lo // 7 : quarter * hi // 7], flip=1) for lo, hi in CUTS
    ]
    down_y = send(down, flip=2)

    seen = [{0: first, 1: send(first, 1)}, {1: send(second, 1, 2), 0: send(second, 0, 2)}]
    seen[0][3], seen[1][3] = send(first, -1), send(second, -1, 2)
    seen, gate_x[0] = together((seen, gate_x[0]))
    seen[0][2], seen[1][2] = send(seen[0][1], 1), send(seen[1][1], 1)
    seen[0][2], seen[1][2], gate_x[1], down_y = together(
        (seen[0][2], seen[1][2], gate_x[1], down_y)
    )

    chosen = jnp.stack([e, e ^ 1]).astype(jnp.int32)
    earlier = jnp.triu(jnp.ones((tok, tok), BF), 1)

    def places(info):
        matches = info[:, None, :top].astype(jnp.int32) == chosen[:, None, None]
        hits = jnp.any(matches, axis=2)
        weight = jnp.sum(jnp.where(matches, info[:, None, top:].astype(F32), 0.0), axis=2)
        rank = jnp.dot(hits.astype(BF), earlier, preferred_element_type=F32)
        rank = jnp.where(hits, rank, -1.0)
        place = (rank[..., None, :] == jnp.arange(slots, dtype=F32)[:, None]).astype(BF)
        pay = place * weight[..., None, :].astype(BF)
        return place, pay.reshape(chips, chunk, tok)

    infos = [jnp.stack([seen[g][k][tok:, :tok] for k in range(chips)]) for g in range(2)]
    helds = [jnp.stack([seen[g][k][:tok] for k in range(chips)]) for g in range(2)]
    info_x = send(infos[0], flip=1)
    place0, pay0 = places(infos[0])
    place1, _ = places(infos[1])
    place1, gate_x[2] = together((place1, gate_x[2]))

    def choose(place, held):
        def of(expert):
            return jnp.einsum(
                "zst,ztk->zsk", place[:, expert], held, preferred_element_type=F32
            ).astype(BF)

        other = send(of(1), core=1)
        return jnp.concatenate([of(0), other], axis=1)

    chosen0, chosen1 = choose(place0, helds[0]), choose(place1, helds[1])
    weights = jnp.concatenate([gate, *gate_x])

    def product(rows):
        flat = rows.reshape(-1, half)
        return jnp.dot(flat, weights, preferred_element_type=F32).reshape(chips, chunk, 2 * ff)

    order = (2, 1, 3, 0)
    sent = product(chosen1).astype(BF)
    sent, chosen0 = together((sent, chosen0))
    part = [send(sent[k], flip=2) for k in order]
    near = product(chosen0)
    pay = jnp.stack([pay0, places(info_x)[1]])

    hidden, away, out = {}, {}, {}

    def finish(q, came):
        gu = near[order[q]] + came.astype(F32)
        own = (jax.nn.silu(gu[:, :ff]) * gu[:, ff:]).astype(BF)
        hidden[q] = (own, send(own, flip=1))

    def down_product(q):
        own = hidden[q][0]
        joined = jnp.concatenate([own, hidden[q][1]])
        value = jnp.concatenate(
            [jnp.dot(joined, w, preferred_element_type=F32).astype(BF) for w in (down, down_y)],
            axis=1,
        ).reshape(2, 2, slots, half)
        out[q], away[q] = value[:, 0], value[:, 1]

    def weigh(q, came):
        rows = jnp.concatenate([out[q], came], axis=1)
        return jnp.einsum("gst,gsk->gtk", pay[:, order[q]], rows, preferred_element_type=F32)

    def before_down(q, value):
        own, value = together((hidden[q][0], value))
        hidden[q] = (own, hidden[q][1])
        return value

    def cross(q):
        return send(away[q], core=1)

    finish(0, part[0])
    down_product(0)
    came, part[1] = together((cross(0), part[1]))
    finish(1, part[1])
    term = weigh(0, came).astype(BF)
    middle = [send(term[g], 1) for g in range(2)]
    middle[0], part[2] = before_down(1, (middle[0], part[2]))
    down_product(1)
    finish(2, part[2])
    part[3] = before_down(2, part[3])
    down_product(2)
    finish(3, part[3])
    down_product(3)
    away[3], came, middle[1] = together((away[3], cross(1), middle[1]))
    term = weigh(1, came).astype(BF)
    back = [send(term[0], -1), send(term[1], -1, 1)]
    term = weigh(2, cross(2))
    term = [(term[g] + middle[g].astype(F32)).astype(BF) for g in range(2)]
    forth = [send(term[0], 1), send(term[1], 1, 1)]
    term = weigh(3, cross(3))
    theirs = send(term[1].astype(BF), flip=1)
    mine = (term[0] + back[0].astype(F32) + forth[0].astype(F32)).astype(BF)
    far = (theirs.astype(F32) + back[1].astype(F32) + forth[1].astype(F32)).astype(BF)

    mixed = jnp.zeros(tokens.shape, BF)
    for r, piece in enumerate(
        [mine[:, :quarter], far[:, :quarter], mine[:, quarter:], far[:, quarter:]]
    ):
        mixed = lax.dynamic_update_slice_in_dim(mixed, piece, (d ^ r) * quarter, axis=1)
    return mixed


def solution(mesh):
    placed = (
        P(("dp", "expert"), None),
        P("expert", "dp", None),
        P("expert", None, "dp"),
        P(("dp", "expert"), None),
        P(("dp", "expert"), None),
    )
    short = mesh.shape["expert"] == 8 and mesh.shape["dp"] == 4
    return jax.shard_map(
        paired if short else gathered,
        mesh=mesh,
        in_specs=placed,
        out_specs=P(("dp", "expert"), None),
        check_vma=False,
    )
```

```python
import jax
import jax.numpy as jnp
from jax import lax
from jax.sharding import PartitionSpec as P

BF = jnp.bfloat16
F32 = jnp.float32
CUTS = ((0, 5), (5, 7))


def gathered(tokens, gate_up, down_proj, expert_ids, gate_weights):
    owners = lax.axis_size("expert")
    tok_rows = tokens.shape[0]
    width = tokens.shape[1]
    hidden_units = down_proj.shape[1]
    slots = 4 * tok_rows // owners
    total_rows = owners * slots
    owner_ids = jnp.arange(owners, dtype=jnp.int32)
    matches = expert_ids[:, :, None] == owner_ids[None, None, :]
    hits = jnp.sum(matches.astype(jnp.int32), axis=1)
    pick_weight = jnp.sum(
        jnp.where(matches, gate_weights[:, :, None].astype(F32), 0.0), axis=1
    )
    before = jnp.cumsum(hits, axis=0) - hits
    target = jnp.where(hits > 0, owner_ids[None, :] * slots + before, -1)
    slot_owner = jnp.arange(total_rows, dtype=jnp.int32) // slots
    slot_ids = jnp.arange(total_rows, dtype=jnp.int32)
    placed = jnp.take(target, slot_owner, axis=1) == slot_ids[None, :]
    place_bf = placed.astype(BF)
    outgoing = jnp.dot(place_bf.T, tokens, preferred_element_type=F32).astype(BF)
    arrived = lax.all_to_all(
        outgoing.reshape(owners, slots, width), "expert", split_axis=0, concat_axis=0, tiled=True
    )
    rows = arrived.reshape(total_rows, width)
    gu = jnp.dot(
        rows,
        lax.all_gather(gate_up, "dp", axis=1, tiled=True)[0],
        preferred_element_type=F32,
    )
    hidden = (jax.nn.silu(gu[:, :hidden_units]) * gu[:, hidden_units:]).astype(BF)
    result = jnp.dot(
        hidden,
        lax.all_gather(down_proj, "dp", axis=2, tiled=True)[0],
        preferred_element_type=F32,
    ).astype(BF)
    returned = lax.all_to_all(
        result.reshape(owners, slots, width), "expert", split_axis=0, concat_axis=0, tiled=True
    )
    weighted = (place_bf.astype(F32) * jnp.take(pick_weight, slot_owner, axis=1)).astype(BF)
    mixed = jnp.dot(weighted, returned.reshape(total_rows, width), preferred_element_type=F32)
    return mixed.astype(BF)


def paired(tokens, gate_up, down_proj, expert_ids, gate_weights):
    owners = lax.axis_size("expert")
    chips = owners // 2
    tok = tokens.shape[0]
    top = expert_ids.shape[1]
    quarter = gate_up.shape[1]
    half = 2 * quarter
    ff = down_proj.shape[1]
    slots = 4 * tok // owners
    chunk = 2 * slots
    d = lax.axis_index("dp")
    e = lax.axis_index("expert")
    gate, down = gate_up[0], down_proj[0]
    together = lax.optimization_barrier

    def send(value, along=0, flip=0, core=0):
        return lax.ppermute(
            value,
            ("dp", "expert"),
            [
                (i * owners + j, (i ^ flip) * owners + ((j ^ core) + 2 * along) % owners)
                for i in range(4)
                for j in range(owners)
            ],
        )

    def depths(r):
        return lax.dynamic_slice_in_dim(tokens, (d ^ r) * quarter, quarter, axis=1)

    info = jnp.concatenate([expert_ids.astype(BF), gate_weights], axis=1).T
    info = jnp.pad(info, ((0, 0), (0, half - tok)))

    def payload(r):
        return jnp.concatenate([jnp.concatenate([depths(r), depths(r + 1)], axis=1), info])

    first, second = payload(0), payload(2)
    gate_x = [
        send(gate[quarter * lo // 7 : quarter * hi // 7], flip=1) for lo, hi in CUTS
    ]
    down_y = send(down, flip=2)

    pair = send(second, flip=2)
    seen = [{0: own, 1: send(own, 1), 3: send(own, -1)} for own in (first, pair)]
    for held in seen:
        held[2] = send(held[1], 1)
    seen[0][2], seen[1][2], seen[1][3], gate_x[0], down_y = together(
        (seen[0][2], seen[1][2], seen[1][3], gate_x[0], down_y)
    )

    chosen = jnp.stack([e, e ^ 1]).astype(jnp.int32)
    earlier = jnp.triu(jnp.ones((tok, tok), BF), 1)

    def places(info):
        matches = info[:, None, :top].astype(jnp.int32) == chosen[:, None, None]
        hits = jnp.any(matches, axis=2)
        weight = jnp.sum(jnp.where(matches, info[:, None, top:].astype(F32), 0.0), axis=2)
        rank = jnp.dot(hits.astype(BF), earlier, preferred_element_type=F32)
        rank = jnp.where(hits, rank, -1.0)
        place = (rank[..., None, :] == jnp.arange(slots, dtype=F32)[:, None]).astype(BF)
        pay = place * weight[..., None, :].astype(BF)
        return place, pay.reshape(chips, chunk, tok)

    infos = [jnp.stack([seen[g][k][tok:, :tok] for k in range(chips)]) for g in range(2)]
    helds = [jnp.stack([seen[g][k][:tok] for k in range(chips)]) for g in range(2)]
    info_x = send(infos[0], flip=1)
    place0, pay0 = places(infos[0])
    place1, _ = places(infos[1])
    place1, gate_x[1] = together((place1, gate_x[1]))

    def choose(place, held):
        def of(expert):
            return jnp.einsum(
                "zst,ztk->zsk", place[:, expert], held, preferred_element_type=F32
            ).astype(BF)

        other = send(of(1), core=1)
        return jnp.concatenate([of(0), other], axis=1)

    chosen0, chosen1 = choose(place0, helds[0]), choose(place1, helds[1])
    weights = jnp.concatenate([gate, *gate_x])

    def product(rows):
        flat = rows.reshape(-1, half)
        return jnp.dot(flat, weights, preferred_element_type=F32).reshape(chips, chunk, 2 * ff)

    order = (2, 1, 3, 0)
    sent = product(chosen1).astype(BF)
    sent, chosen0 = together((sent, chosen0))
    part = [send(sent[k], flip=2) for k in order]
    near = product(chosen0)
    near, info_x = together((near, info_x))
    pay = jnp.stack([pay0, places(info_x)[1]])

    hidden, away, out = {}, {}, {}

    def finish(q, came):
        gu = near[order[q]] + came.astype(F32)
        own = (jax.nn.silu(gu[:, :ff]) * gu[:, ff:]).astype(BF)
        hidden[q] = (own, send(own, flip=1))

    def down_product(q):
        own = hidden[q][0]
        joined = jnp.concatenate([own, hidden[q][1]])
        value = jnp.concatenate(
            [jnp.dot(joined, w, preferred_element_type=F32).astype(BF) for w in (down, down_y)],
            axis=1,
        ).reshape(2, 2, slots, half)
        out[q], away[q] = value[:, 0], value[:, 1]

    def weigh(q, came):
        rows = jnp.concatenate([out[q], came], axis=1)
        return jnp.einsum("gst,gsk->gtk", pay[:, order[q]], rows, preferred_element_type=F32)

    def before_down(q, value):
        own, value = together((hidden[q][0], value))
        hidden[q] = (own, hidden[q][1])
        return value

    def cross(q):
        return send(away[q], core=1)

    finish(0, part[0])
    down_product(0)
    came, part[1] = together((cross(0), part[1]))
    finish(1, part[1])
    term = weigh(0, came).astype(BF)
    middle = [send(term[g], 1) for g in range(2)]
    middle[0], part[2] = before_down(1, (middle[0], part[2]))
    down_product(1)
    finish(2, part[2])
    part[3] = before_down(2, part[3])
    down_product(2)
    finish(3, part[3])
    down_product(3)
    away[3], came, middle[1] = together((away[3], cross(1), middle[1]))
    term = weigh(1, came).astype(BF)
    back = [send(term[0], -1), send(term[1], -1, 1)]
    term = weigh(2, cross(2))
    term = [(term[g] + middle[g].astype(F32)).astype(BF) for g in range(2)]
    forth = [send(term[0], 1), send(term[1], 1, 1)]
    term = weigh(3, cross(3))
    theirs = send(term[1].astype(BF), flip=1)
    mine = (term[0] + back[0].astype(F32) + forth[0].astype(F32)).astype(BF)
    far = (theirs.astype(F32) + back[1].astype(F32) + forth[1].astype(F32)).astype(BF)

    mixed = jnp.zeros(tokens.shape, BF)
    for r, piece in enumerate(
        [mine[:, :quarter], far[:, :quarter], mine[:, quarter:], far[:, quarter:]]
    ):
        mixed = lax.dynamic_update_slice_in_dim(mixed, piece, (d ^ r) * quarter, axis=1)
    return mixed


def solution(mesh):
    placed = (
        P(("dp", "expert"), None),
        P("expert", "dp", None),
        P("expert", None, "dp"),
        P(("dp", "expert"), None),
        P(("dp", "expert"), None),
    )
    short = mesh.shape["expert"] == 8 and mesh.shape["dp"] == 4
    return jax.shard_map(
        paired if short else gathered,
        mesh=mesh,
        in_specs=placed,
        out_specs=P(("dp", "expert"), None),
        check_vma=False,
    )
```

```python
import jax
import jax.numpy as jnp
from jax import lax
from jax.sharding import PartitionSpec as P

BF = jnp.bfloat16
F32 = jnp.float32

def gathered(tokens, gate_up, down_proj, expert_ids, gate_weights):
    owners = lax.axis_size("expert")
    tok_rows = tokens.shape[0]
    width = tokens.shape[1]
    hidden_units = down_proj.shape[1]
    slots = 4 * tok_rows // owners
    total_rows = owners * slots
    owner_ids = jnp.arange(owners, dtype=jnp.int32)
    matches = expert_ids[:, :, None] == owner_ids[None, None, :]
    hits = jnp.sum(matches.astype(jnp.int32), axis=1)
    pick_weight = jnp.sum(
        jnp.where(matches, gate_weights[:, :, None].astype(F32), 0.0), axis=1
    )
    before = jnp.cumsum(hits, axis=0) - hits
    target = jnp.where(hits > 0, owner_ids[None, :] * slots + before, -1)
    slot_owner = jnp.arange(total_rows, dtype=jnp.int32) // slots
    slot_ids = jnp.arange(total_rows, dtype=jnp.int32)
    placed = jnp.take(target, slot_owner, axis=1) == slot_ids[None, :]
    place_bf = placed.astype(BF)
    outgoing = jnp.dot(place_bf.T, tokens, preferred_element_type=F32).astype(BF)
    arrived = lax.all_to_all(
        outgoing.reshape(owners, slots, width), "expert", split_axis=0, concat_axis=0, tiled=True
    )
    rows = arrived.reshape(total_rows, width)
    gu = jnp.dot(
        rows,
        lax.all_gather(gate_up, "dp", axis=1, tiled=True)[0],
        preferred_element_type=F32,
    )
    hidden = (jax.nn.silu(gu[:, :hidden_units]) * gu[:, hidden_units:]).astype(BF)
    result = jnp.dot(
        hidden,
        lax.all_gather(down_proj, "dp", axis=2, tiled=True)[0],
        preferred_element_type=F32,
    ).astype(BF)
    returned = lax.all_to_all(
        result.reshape(owners, slots, width), "expert", split_axis=0, concat_axis=0, tiled=True
    )
    weighted = (place_bf.astype(F32) * jnp.take(pick_weight, slot_owner, axis=1)).astype(BF)
    mixed = jnp.dot(weighted, returned.reshape(total_rows, width), preferred_element_type=F32)
    return mixed.astype(BF)


def paired(tokens, gate_up, down_proj, expert_ids, gate_weights):
    owners = lax.axis_size("expert")
    chips = owners // 2
    tok = tokens.shape[0]
    quarter = gate_up.shape[1]
    half = 2 * quarter
    ff = down_proj.shape[1]
    slots = 4 * tok // owners
    chunk = 2 * slots
    d = lax.axis_index("dp")
    e = lax.axis_index("expert")
    gate, down = gate_up[0], down_proj[0]
    together = lax.optimization_barrier

    def send(value, along=0, flip=0, core=0):
        return lax.ppermute(
            value,
            ("dp", "expert"),
            [
                (i * owners + j, (i ^ flip) * owners + ((j ^ core) + 2 * along) % owners)
                for i in range(4)
                for j in range(owners)
            ],
        )

    def depths(r):
        return lax.dynamic_slice_in_dim(tokens, (d ^ r) * quarter, quarter, axis=1)

    info = jnp.concatenate([expert_ids.T.astype(BF), gate_weights.T], axis=1)
    info = jnp.pad(info, ((0, 0), (0, half - 2 * tok)))

    def payload(r):
        return jnp.concatenate([jnp.concatenate([depths(r), depths(r + 1)], axis=1), info])

    first, second = payload(0), payload(2)
    gate_x = send(gate, flip=1)
    down_y = send(down, flip=2)

    pair = send(second, flip=2)
    seen = [{0: own, 1: send(own, 1), 3: send(own, -1)} for own in (first, pair)]
    for held in seen:
        held[2] = send(held[1], 1)
    seen[1][2], down_y = together((seen[1][2], down_y))

    chosen = jnp.stack([e, e ^ 1]).astype(jnp.int32)
    earlier = jnp.triu(jnp.ones((tok, tok), BF), 1)

    def places(info):
        matches = info[:, None, :, :tok].astype(jnp.int32) == chosen[:, None, None]
        hits = jnp.any(matches, axis=2)
        weight = jnp.sum(jnp.where(matches, info[:, None, :, tok:].astype(F32), 0.0), axis=2)
        rank = jnp.dot(hits.astype(BF), earlier, preferred_element_type=F32)
        rank = jnp.where(hits, rank, -1.0)
        place = (rank[..., None, :] == jnp.arange(slots, dtype=F32)[:, None]).astype(BF)
        pay = place * weight[..., None, :].astype(BF)
        return place, pay.reshape(chips, chunk, tok)

    infos = [jnp.stack([seen[g][k][tok:, : 2 * tok] for k in range(chips)]) for g in range(2)]
    helds = [jnp.stack([seen[g][k][:tok] for k in range(chips)]) for g in range(2)]
    info_x = send(infos[0], flip=1)
    place0, pay0 = places(infos[0])
    place1, _ = places(infos[1])

    def choose(place, held):
        def of(expert):
            return jnp.einsum(
                "zst,ztk->zsk", place[:, expert], held, preferred_element_type=F32
            ).astype(BF)

        other = send(of(1), core=1)
        return jnp.concatenate([of(0), other], axis=1)

    chosen0, chosen1 = choose(place0, helds[0]), choose(place1, helds[1])
    downs = jnp.concatenate([down, down_y], axis=1)
    chosen1, gate_x, downs = together((chosen1, gate_x, downs))
    weights = jnp.concatenate([gate, gate_x])

    def product(rows):
        flat = rows.reshape(-1, half)
        return jnp.dot(flat, weights, preferred_element_type=F32).reshape(chips, chunk, 2 * ff)

    order = (2, 1, 3, 0)
    sent = product(chosen1).astype(BF)
    sent, chosen0 = together((sent, chosen0))
    part = [send(sent[k], flip=2) for k in order]
    near = product(chosen0)
    near, info_x = together((near, info_x))
    pay = jnp.stack([pay0, places(info_x)[1]])

    hidden, away, out = {}, {}, {}

    def finish(q, came):
        gu = near[order[q]] + came.astype(F32)
        own = (jax.nn.silu(gu[:, :ff]) * gu[:, ff:]).astype(BF)
        hidden[q] = (own, send(own, flip=1))

    def down_product(q):
        own = hidden[q][0]
        joined = jnp.concatenate([own, hidden[q][1]])
        value = jnp.dot(joined, downs, preferred_element_type=F32).astype(BF)
        value = value.reshape(2, 2, slots, half)
        out[q], away[q] = value[:, 0], value[:, 1]

    def weigh(q, came):
        rows = jnp.concatenate([out[q], came], axis=1)
        return jnp.einsum("gst,gsk->gtk", pay[:, order[q]], rows, preferred_element_type=F32)

    def before_down(q, value):
        own, value = together((hidden[q][0], value))
        hidden[q] = (own, hidden[q][1])
        return value

    def cross(q):
        return send(away[q], core=1)

    finish(0, part[0])
    down_product(0)
    came, part[1] = together((cross(0), part[1]))
    finish(1, part[1])
    term = weigh(0, came).astype(BF)
    middle = [send(term[g], 1) for g in range(2)]
    middle[0], part[2] = before_down(1, (middle[0], part[2]))
    down_product(1)
    finish(2, part[2])
    part[3] = before_down(2, part[3])
    down_product(2)
    finish(3, part[3])
    down_product(3)
    away[3], came, middle[1] = together((away[3], cross(1), middle[1]))
    term = weigh(1, came).astype(BF)
    back = [send(term[0], -1), send(term[1], -1, 1)]
    term = weigh(2, cross(2))
    term = [(term[g] + middle[g].astype(F32)).astype(BF) for g in range(2)]
    forth = [send(term[0], 1), send(term[1], 1, 1)]
    term = weigh(3, cross(3))
    theirs = send(term[1].astype(BF), flip=1)
    mine = (term[0] + back[0].astype(F32) + forth[0].astype(F32)).astype(BF)
    far = (theirs.astype(F32) + back[1].astype(F32) + forth[1].astype(F32)).astype(BF)

    mixed = jnp.zeros(tokens.shape, BF)
    for r, piece in enumerate(
        [mine[:, :quarter], far[:, :quarter], mine[:, quarter:], far[:, quarter:]]
    ):
        mixed = lax.dynamic_update_slice_in_dim(mixed, piece, (d ^ r) * quarter, axis=1)
    return mixed


def solution(mesh):
    placed = (
        P(("dp", "expert"), None),
        P("expert", "dp", None),
        P("expert", None, "dp"),
        P(("dp", "expert"), None),
        P(("dp", "expert"), None),
    )
    short = mesh.shape["expert"] == 8 and mesh.shape["dp"] == 4
    return jax.shard_map(
        paired if short else gathered,
        mesh=mesh,
        in_specs=placed,
        out_specs=P(("dp", "expert"), None),
        check_vma=False,
    )
```

```python
import jax
import jax.numpy as jnp
from jax import lax
from jax.sharding import PartitionSpec as P

BF = jnp.bfloat16
F32 = jnp.float32

def gathered(tokens, gate_up, down_proj, expert_ids, gate_weights):
    owners = lax.axis_size("expert")
    tok_rows = tokens.shape[0]
    width = tokens.shape[1]
    hidden_units = down_proj.shape[1]
    slots = 4 * tok_rows // owners
    total_rows = owners * slots
    owner_ids = jnp.arange(owners, dtype=jnp.int32)
    matches = expert_ids[:, :, None] == owner_ids[None, None, :]
    hits = jnp.sum(matches.astype(jnp.int32), axis=1)
    pick_weight = jnp.sum(
        jnp.where(matches, gate_weights[:, :, None].astype(F32), 0.0), axis=1
    )
    before = jnp.cumsum(hits, axis=0) - hits
    target = jnp.where(hits > 0, owner_ids[None, :] * slots + before, -1)
    slot_owner = jnp.arange(total_rows, dtype=jnp.int32) // slots
    slot_ids = jnp.arange(total_rows, dtype=jnp.int32)
    placed = jnp.take(target, slot_owner, axis=1) == slot_ids[None, :]
    place_bf = placed.astype(BF)
    outgoing = jnp.dot(place_bf.T, tokens, preferred_element_type=F32).astype(BF)
    arrived = lax.all_to_all(
        outgoing.reshape(owners, slots, width), "expert", split_axis=0, concat_axis=0, tiled=True
    )
    rows = arrived.reshape(total_rows, width)
    gu = jnp.dot(
        rows,
        lax.all_gather(gate_up, "dp", axis=1, tiled=True)[0],
        preferred_element_type=F32,
    )
    hidden = (jax.nn.silu(gu[:, :hidden_units]) * gu[:, hidden_units:]).astype(BF)
    result = jnp.dot(
        hidden,
        lax.all_gather(down_proj, "dp", axis=2, tiled=True)[0],
        preferred_element_type=F32,
    ).astype(BF)
    returned = lax.all_to_all(
        result.reshape(owners, slots, width), "expert", split_axis=0, concat_axis=0, tiled=True
    )
    weighted = (place_bf.astype(F32) * jnp.take(pick_weight, slot_owner, axis=1)).astype(BF)
    mixed = jnp.dot(weighted, returned.reshape(total_rows, width), preferred_element_type=F32)
    return mixed.astype(BF)


def paired(tokens, gate_up, down_proj, expert_ids, gate_weights):
    owners = lax.axis_size("expert")
    chips = owners // 2
    tok = tokens.shape[0]
    quarter = gate_up.shape[1]
    half = 2 * quarter
    ff = down_proj.shape[1]
    slots = 4 * tok // owners
    chunk = 2 * slots
    d = lax.axis_index("dp")
    e = lax.axis_index("expert")
    gate, down = gate_up[0], down_proj[0]
    together = lax.optimization_barrier

    def send(value, along=0, flip=0, core=0):
        return lax.ppermute(
            value,
            ("dp", "expert"),
            [
                (i * owners + j, (i ^ flip) * owners + ((j ^ core) + 2 * along) % owners)
                for i in range(4)
                for j in range(owners)
            ],
        )

    def depths(r):
        return lax.dynamic_slice_in_dim(tokens, (d ^ r) * quarter, quarter, axis=1)

    info = jnp.concatenate([expert_ids.T.astype(BF), gate_weights.T], axis=1)
    info = jnp.pad(info, ((0, 0), (0, half - 2 * tok)))

    def payload(r):
        return jnp.concatenate([jnp.concatenate([depths(r), depths(r + 1)], axis=1), info])

    first, second = payload(0), payload(2)
    gate_x = send(gate, flip=1)

    seen = [{0: first, 1: send(first, 1)}, {0: send(second, flip=2)}]
    seen[0][0], seen[1][0], down = together((seen[0][0], seen[1][0], down))
    down_y = send(down, flip=2)
    seen[1][1] = send(seen[1][0], 1)
    for held in seen:
        held[3] = send(held[0], -1)
        held[2] = send(held[1], 1)
    downs = jnp.concatenate([down, down_y], axis=1)
    seen[1][2], downs = together((seen[1][2], downs))

    chosen = jnp.stack([e, e ^ 1]).astype(jnp.int32)
    earlier = jnp.triu(jnp.ones((tok, tok), BF), 1)

    def places(info):
        matches = info[:, None, :, :tok].astype(jnp.int32) == chosen[:, None, None]
        hits = jnp.any(matches, axis=2)
        weight = jnp.sum(jnp.where(matches, info[:, None, :, tok:].astype(F32), 0.0), axis=2)
        rank = jnp.dot(hits.astype(BF), earlier, preferred_element_type=F32)
        rank = jnp.where(hits, rank, -1.0)
        place = (rank[..., None, :] == jnp.arange(slots, dtype=F32)[:, None]).astype(BF)
        pay = place * weight[..., None, :].astype(BF)
        return place, pay.reshape(chips, chunk, tok)

    infos = [jnp.stack([seen[g][k][tok:, : 2 * tok] for k in range(chips)]) for g in range(2)]
    helds = [jnp.stack([seen[g][k][:tok] for k in range(chips)]) for g in range(2)]
    info_x = send(infos[0], flip=1)
    place0, pay0 = places(infos[0])
    place1, _ = places(infos[1])

    def choose(place, held):
        def of(expert):
            return jnp.einsum(
                "zst,ztk->zsk", place[:, expert], held, preferred_element_type=F32
            ).astype(BF)

        other = send(of(1), core=1)
        return jnp.concatenate([of(0), other], axis=1)

    chosen0, chosen1 = choose(place0, helds[0]), choose(place1, helds[1])

    chosen1, gate_x = together((chosen1, gate_x))
    weights = jnp.concatenate([gate, gate_x])

    def product(rows):
        flat = rows.reshape(-1, half)
        return jnp.dot(flat, weights, preferred_element_type=F32).reshape(chips, chunk, 2 * ff)

    order = (2, 1, 3, 0)
    sent = product(chosen1).astype(BF)
    sent, chosen0 = together((sent, chosen0))
    part = [send(sent[k], flip=2) for k in order]
    near = product(chosen0)
    near, info_x = together((near, info_x))
    pays = [pay0, places(info_x)[1]]

    hidden, out, came = {}, {}, {}

    def finish(q):
        gu = near[order[q]] + part[q].astype(F32)
        own = (jax.nn.silu(gu[:, :ff]) * gu[:, ff:]).astype(BF)
        hidden[q, 0], hidden[q, 1] = own, send(own, flip=1)

    def down_product(q, g):
        value = jnp.dot(hidden[q, g], downs, preferred_element_type=F32).astype(BF)
        value = value.reshape(2, slots, half)
        out[q, g], came[q, g] = value[0], send(value[1], core=1)

    def weigh(q, g):
        rows = jnp.concatenate([out[q, g], came[q, g]])
        return lax.dot_general(
            pays[g][order[q]], rows, (((0,), (0,)), ((), ())), preferred_element_type=F32
        )

    def before_weigh(q, value):
        came[q, 1], value = together((came[q, 1], value))
        return value

    def before_down(q, value):
        hidden[q, 1], value = together((hidden[q, 1], value))
        return value

    middle, back, forth = {}, {}, {}
    finish(0)
    down_product(0, 0)
    middle[0] = send(weigh(0, 0).astype(BF), 1)
    down_product(0, 1)
    middle[0], part[1] = before_weigh(0, (middle[0], part[1]))
    middle[1] = send(weigh(0, 1).astype(BF), 1)
    finish(1)
    down_product(1, 0)
    back[0] = send(weigh(1, 0).astype(BF), -1)
    part[2] = before_down(1, part[2])
    down_product(1, 1)
    middle[1] = before_weigh(1, middle[1])
    back[1] = send(weigh(1, 1).astype(BF), -1, 1)
    finish(2)
    down_product(2, 0)
    forth[0] = send((weigh(2, 0) + middle[0].astype(F32)).astype(BF), 1)
    part[3] = before_down(2, part[3])
    down_product(2, 1)
    back[0] = before_weigh(2, back[0])
    forth[1] = send((weigh(2, 1) + middle[1].astype(F32)).astype(BF), 1, 1)
    finish(3)
    down_product(3, 0)
    down_product(3, 1)
    back[1] = before_weigh(3, back[1])
    term = [weigh(3, g) for g in range(2)]
    theirs = send(term[1].astype(BF), flip=1)
    mine = (term[0] + back[0].astype(F32) + forth[0].astype(F32)).astype(BF)
    far = (theirs.astype(F32) + back[1].astype(F32) + forth[1].astype(F32)).astype(BF)

    mixed = jnp.zeros(tokens.shape, BF)
    for r, piece in enumerate(
        [mine[:, :quarter], far[:, :quarter], mine[:, quarter:], far[:, quarter:]]
    ):
        mixed = lax.dynamic_update_slice_in_dim(mixed, piece, (d ^ r) * quarter, axis=1)
    return mixed


def solution(mesh):
    placed = (
        P(("dp", "expert"), None),
        P("expert", "dp", None),
        P("expert", None, "dp"),
        P(("dp", "expert"), None),
        P(("dp", "expert"), None),
    )
    short = mesh.shape["expert"] == 8 and mesh.shape["dp"] == 4
    return jax.shard_map(
        paired if short else gathered,
        mesh=mesh,
        in_specs=placed,
        out_specs=P(("dp", "expert"), None),
        check_vma=False,
    )
```

```python
import jax
import jax.numpy as jnp
from jax import lax
from jax.sharding import PartitionSpec as P

BF = jnp.bfloat16
F32 = jnp.float32

def gathered(tokens, gate_up, down_proj, expert_ids, gate_weights):
    owners = lax.axis_size("expert")
    tok_rows = tokens.shape[0]
    width = tokens.shape[1]
    hidden_units = down_proj.shape[1]
    slots = 4 * tok_rows // owners
    total_rows = owners * slots
    owner_ids = jnp.arange(owners, dtype=jnp.int32)
    matches = expert_ids[:, :, None] == owner_ids[None, None, :]
    hits = jnp.sum(matches.astype(jnp.int32), axis=1)
    pick_weight = jnp.sum(
        jnp.where(matches, gate_weights[:, :, None].astype(F32), 0.0), axis=1
    )
    before = jnp.cumsum(hits, axis=0) - hits
    target = jnp.where(hits > 0, owner_ids[None, :] * slots + before, -1)
    slot_owner = jnp.arange(total_rows, dtype=jnp.int32) // slots
    slot_ids = jnp.arange(total_rows, dtype=jnp.int32)
    placed = jnp.take(target, slot_owner, axis=1) == slot_ids[None, :]
    place_bf = placed.astype(BF)
    outgoing = jnp.dot(place_bf.T, tokens, preferred_element_type=F32).astype(BF)
    arrived = lax.all_to_all(
        outgoing.reshape(owners, slots, width), "expert", split_axis=0, concat_axis=0, tiled=True
    )
    rows = arrived.reshape(total_rows, width)
    gu = jnp.dot(
        rows,
        lax.all_gather(gate_up, "dp", axis=1, tiled=True)[0],
        preferred_element_type=F32,
    )
    hidden = (jax.nn.silu(gu[:, :hidden_units]) * gu[:, hidden_units:]).astype(BF)
    result = jnp.dot(
        hidden,
        lax.all_gather(down_proj, "dp", axis=2, tiled=True)[0],
        preferred_element_type=F32,
    ).astype(BF)
    returned = lax.all_to_all(
        result.reshape(owners, slots, width), "expert", split_axis=0, concat_axis=0, tiled=True
    )
    weighted = (place_bf.astype(F32) * jnp.take(pick_weight, slot_owner, axis=1)).astype(BF)
    mixed = jnp.dot(weighted, returned.reshape(total_rows, width), preferred_element_type=F32)
    return mixed.astype(BF)


def paired(tokens, gate_up, down_proj, expert_ids, gate_weights):
    owners = lax.axis_size("expert")
    chips = owners // 2
    tok = tokens.shape[0]
    quarter = gate_up.shape[1]
    half = 2 * quarter
    ff = down_proj.shape[1]
    slots = 4 * tok // owners
    chunk = 2 * slots
    d = lax.axis_index("dp")
    e = lax.axis_index("expert")
    gate, down = gate_up[0], down_proj[0]
    together = lax.optimization_barrier

    def send(value, along=0, flip=0, core=0):
        return lax.ppermute(
            value,
            ("dp", "expert"),
            [
                (i * owners + j, (i ^ flip) * owners + ((j ^ core) + 2 * along) % owners)
                for i in range(4)
                for j in range(owners)
            ],
        )

    def depths(r):
        return lax.dynamic_slice_in_dim(tokens, (d ^ r) * quarter, quarter, axis=1)

    info = jnp.concatenate([expert_ids.T.astype(BF), gate_weights.T], axis=1)
    info = jnp.pad(info, ((0, 0), (0, half - 2 * tok)))

    def payload(r):
        return jnp.concatenate([jnp.concatenate([depths(r), depths(r + 1)], axis=1), info])

    first, second = payload(0), payload(2)
    gate_x = send(gate, flip=1)

    seen = [{0: first, 1: send(first, 1)}, {0: send(second, flip=2)}]
    seen[0][0], seen[1][0], down = together((seen[0][0], seen[1][0], down))
    down_y = send(down, flip=2)
    seen[1][1] = send(seen[1][0], 1)
    for held in seen:
        held[3] = send(held[0], -1)
        held[2] = send(held[1], 1)
    downs = jnp.concatenate([down, down_y], axis=1)
    seen[1][2], downs = together((seen[1][2], downs))

    chosen = jnp.stack([e, e ^ 1]).astype(jnp.int32)
    earlier = jnp.triu(jnp.ones((tok, tok), BF), 1)

    def places(info):
        matches = info[:, None, :, :tok].astype(jnp.int32) == chosen[:, None, None]
        hits = jnp.any(matches, axis=2)
        weight = jnp.sum(jnp.where(matches, info[:, None, :, tok:].astype(F32), 0.0), axis=2)
        rank = jnp.dot(hits.astype(BF), earlier, preferred_element_type=F32)
        rank = jnp.where(hits, rank, -1.0)
        place = (rank[..., None, :] == jnp.arange(slots, dtype=F32)[:, None]).astype(BF)
        pay = place * weight[..., None, :].astype(BF)
        return place, pay.reshape(chips, chunk, tok)

    infos = [jnp.stack([seen[g][k][tok:, : 2 * tok] for k in range(chips)]) for g in range(2)]
    helds = [jnp.stack([seen[g][k][:tok] for k in range(chips)]) for g in range(2)]
    info_x = send(infos[0], flip=1)
    place0, pay0 = places(infos[0])
    place1, _ = places(infos[1])

    def choose(place, held):
        def of(expert):
            return jnp.einsum(
                "zst,ztk->zsk", place[:, expert], held, preferred_element_type=F32
            ).astype(BF)

        other = send(of(1), core=1)
        return jnp.concatenate([of(0), other], axis=1)

    chosen0, chosen1 = choose(place0, helds[0]), choose(place1, helds[1])

    chosen1, gate_x = together((chosen1, gate_x))
    weights = jnp.concatenate([gate, gate_x])

    def product(rows):
        flat = rows.reshape(-1, half)
        return jnp.dot(flat, weights, preferred_element_type=F32).reshape(chips, chunk, 2 * ff)

    order = (2, 1, 0, 3)
    sent = product(chosen1).astype(BF)
    sent, chosen0 = together((sent, chosen0))
    sent = [sent[k] for k in order]
    part = [send(value, flip=2) for value in sent[:2]]
    near = product(chosen0)
    pays = [pay0]

    hidden, out, came = {}, {}, {}

    def finish(q):
        gu = near[order[q]] + part[q].astype(F32)
        own = (jax.nn.silu(gu[:, :ff]) * gu[:, ff:]).astype(BF)
        hidden[q, 0], hidden[q, 1] = own, send(own, flip=1)

    def down_product(q, g):
        value = jnp.dot(hidden[q, g], downs, preferred_element_type=F32).astype(BF)
        value = value.reshape(2, slots, half)
        out[q, g], came[q, g] = value[0], send(value[1], core=1)

    def weigh(q, g):
        rows = jnp.concatenate([out[q, g], came[q, g]])
        return lax.dot_general(
            pays[g][order[q]], rows, (((0,), (0,)), ((), ())), preferred_element_type=F32
        )

    def before_weigh(q, value):
        came[q, 1], value = together((came[q, 1], value))
        return value

    def before_down(q, value):
        hidden[q, 1], value = together((hidden[q, 1], value))
        return value

    middle, back, forth = {}, {}, {}
    finish(0)
    down_product(0, 0)
    hidden[0, 1], info_x = together((hidden[0, 1], info_x))
    pays.append(places(info_x)[1])
    middle[0] = weigh(0, 0).astype(BF)
    middle[0], sent = together((middle[0], sent))
    part += [send(value, flip=2) for value in sent[2:]]
    middle[0] = send(middle[0], 1)
    down_product(0, 1)
    middle[0], part[1] = before_weigh(0, (middle[0], part[1]))
    middle[1] = send(weigh(0, 1).astype(BF), 1)
    finish(1)
    down_product(1, 0)
    back[0] = send(weigh(1, 0).astype(BF), -1)
    part[2] = before_down(1, part[2])
    down_product(1, 1)
    middle[1] = before_weigh(1, middle[1])
    back[1] = send(weigh(1, 1).astype(BF), -1, 1)
    finish(2)
    down_product(2, 0)
    part[3] = before_down(2, part[3])
    down_product(2, 1)
    finish(3)
    down_product(3, 0)
    forth[0] = send((weigh(3, 0) + middle[0].astype(F32)).astype(BF), 1)
    hidden[3, 1] = before_weigh(2, hidden[3, 1])
    term = [weigh(2, g) for g in range(2)]
    theirs = send(term[1].astype(BF), flip=1)
    down_product(3, 1)
    back = before_weigh(3, back)
    forth[1] = send((weigh(3, 1) + middle[1].astype(F32)).astype(BF), 1, 1)
    mine = (term[0] + back[0].astype(F32) + forth[0].astype(F32)).astype(BF)
    far = (theirs.astype(F32) + back[1].astype(F32) + forth[1].astype(F32)).astype(BF)

    mixed = jnp.zeros(tokens.shape, BF)
    for r, piece in enumerate(
        [mine[:, :quarter], far[:, :quarter], mine[:, quarter:], far[:, quarter:]]
    ):
        mixed = lax.dynamic_update_slice_in_dim(mixed, piece, (d ^ r) * quarter, axis=1)
    return mixed


def solution(mesh):
    placed = (
        P(("dp", "expert"), None),
        P("expert", "dp", None),
        P("expert", None, "dp"),
        P(("dp", "expert"), None),
        P(("dp", "expert"), None),
    )
    short = mesh.shape["expert"] == 8 and mesh.shape["dp"] == 4
    return jax.shard_map(
        paired if short else gathered,
        mesh=mesh,
        in_specs=placed,
        out_specs=P(("dp", "expert"), None),
        check_vma=False,
    )
```

```python
import jax
import jax.numpy as jnp
from jax import lax
from jax.sharding import PartitionSpec as P

BF = jnp.bfloat16
F32 = jnp.float32

def gathered(tokens, gate_up, down_proj, expert_ids, gate_weights):
    owners = lax.axis_size("expert")
    tok_rows = tokens.shape[0]
    width = tokens.shape[1]
    hidden_units = down_proj.shape[1]
    slots = 4 * tok_rows // owners
    total_rows = owners * slots
    owner_ids = jnp.arange(owners, dtype=jnp.int32)
    matches = expert_ids[:, :, None] == owner_ids[None, None, :]
    hits = jnp.sum(matches.astype(jnp.int32), axis=1)
    pick_weight = jnp.sum(
        jnp.where(matches, gate_weights[:, :, None].astype(F32), 0.0), axis=1
    )
    before = jnp.cumsum(hits, axis=0) - hits
    target = jnp.where(hits > 0, owner_ids[None, :] * slots + before, -1)
    slot_owner = jnp.arange(total_rows, dtype=jnp.int32) // slots
    slot_ids = jnp.arange(total_rows, dtype=jnp.int32)
    placed = jnp.take(target, slot_owner, axis=1) == slot_ids[None, :]
    place_bf = placed.astype(BF)
    outgoing = jnp.dot(place_bf.T, tokens, preferred_element_type=F32).astype(BF)
    arrived = lax.all_to_all(
        outgoing.reshape(owners, slots, width), "expert", split_axis=0, concat_axis=0, tiled=True
    )
    rows = arrived.reshape(total_rows, width)
    gu = jnp.dot(
        rows,
        lax.all_gather(gate_up, "dp", axis=1, tiled=True)[0],
        preferred_element_type=F32,
    )
    hidden = (jax.nn.silu(gu[:, :hidden_units]) * gu[:, hidden_units:]).astype(BF)
    result = jnp.dot(
        hidden,
        lax.all_gather(down_proj, "dp", axis=2, tiled=True)[0],
        preferred_element_type=F32,
    ).astype(BF)
    returned = lax.all_to_all(
        result.reshape(owners, slots, width), "expert", split_axis=0, concat_axis=0, tiled=True
    )
    weighted = (place_bf.astype(F32) * jnp.take(pick_weight, slot_owner, axis=1)).astype(BF)
    mixed = jnp.dot(weighted, returned.reshape(total_rows, width), preferred_element_type=F32)
    return mixed.astype(BF)


def paired(tokens, gate_up, down_proj, expert_ids, gate_weights):
    owners = lax.axis_size("expert")
    chips = owners // 2
    tok = tokens.shape[0]
    quarter = gate_up.shape[1]
    half = 2 * quarter
    ff = down_proj.shape[1]
    slots = 4 * tok // owners
    chunk = 2 * slots
    d = lax.axis_index("dp")
    e = lax.axis_index("expert")
    gate, down = gate_up[0], down_proj[0]
    together = lax.optimization_barrier

    def send(value, along=0, flip=0, core=0):
        return lax.ppermute(
            value,
            ("dp", "expert"),
            [
                (i * owners + j, (i ^ flip) * owners + ((j ^ core) + 2 * along) % owners)
                for i in range(4)
                for j in range(owners)
            ],
        )

    def depths(r):
        return lax.dynamic_slice_in_dim(tokens, (d ^ r) * quarter, quarter, axis=1)

    info = jnp.concatenate([expert_ids.T.astype(BF), gate_weights.T], axis=1)
    info = jnp.pad(info, ((0, 0), (0, half - 2 * tok)))

    def payload(r):
        return jnp.concatenate([jnp.concatenate([depths(r), depths(r + 1)], axis=1), info])

    first, second = payload(0), payload(2)
    gate_x = send(gate, flip=1)

    seen = [{0: first, 1: send(first, 1)}, {0: send(second, flip=2)}]
    seen[0][0], seen[1][0], down = together((seen[0][0], seen[1][0], down))
    down_y = send(down, flip=2)
    seen[1][1] = send(seen[1][0], 1)
    for held in seen:
        held[3] = send(held[0], -1)
        held[2] = send(held[1], 1)
    downs = jnp.concatenate([down, down_y], axis=1)
    seen[1][2], downs = together((seen[1][2], downs))

    chosen = jnp.stack([e, e ^ 1]).astype(jnp.int32)
    earlier = jnp.triu(jnp.ones((tok, tok), BF), 1)

    def places(info):
        matches = info[:, None, :, :tok].astype(jnp.int32) == chosen[:, None, None]
        hits = jnp.any(matches, axis=2)
        weight = jnp.sum(jnp.where(matches, info[:, None, :, tok:].astype(F32), 0.0), axis=2)
        rank = jnp.dot(hits.astype(BF), earlier, preferred_element_type=F32)
        rank = jnp.where(hits, rank, -1.0)
        place = (rank[..., None, :] == jnp.arange(slots, dtype=F32)[:, None]).astype(BF)
        pay = place * weight[..., None, :].astype(BF)
        return place, pay.reshape(chips, chunk, tok)

    infos = [jnp.stack([seen[g][k][tok:, : 2 * tok] for k in range(chips)]) for g in range(2)]
    helds = [jnp.stack([seen[g][k][:tok] for k in range(chips)]) for g in range(2)]
    info_x = send(infos[0], flip=1)
    place0, pay0 = places(infos[0])
    place1, _ = places(infos[1])

    def choose(place, held):
        def of(expert):
            return jnp.einsum(
                "zst,ztk->zsk", place[:, expert], held, preferred_element_type=F32
            ).astype(BF)

        other = send(of(1), core=1)
        return jnp.concatenate([of(0), other], axis=1)

    chosen0, chosen1 = choose(place0, helds[0]), choose(place1, helds[1])

    chosen1, gate_x = together((chosen1, gate_x))
    weights = jnp.concatenate([gate, gate_x])

    def product(rows):
        flat = rows.reshape(-1, half)
        return jnp.dot(flat, weights, preferred_element_type=F32).reshape(chips, chunk, 2 * ff)

    order = (2, 1, 0, 3)
    sent = product(chosen1).astype(BF)
    sent, chosen0 = together((sent, chosen0))
    sent = [sent[k] for k in order]
    part = [send(value, flip=2) for value in sent[:2]]
    near = product(chosen0)
    pays = [pay0]

    hidden, out, came = {}, {}, {}

    def finish(q):
        gu = near[order[q]] + part[q].astype(F32)
        own = (jax.nn.silu(gu[:, :ff]) * gu[:, ff:]).astype(BF)
        hidden[q, 0], hidden[q, 1] = own, send(own, flip=1)

    def down_product(q, g):
        value = jnp.dot(hidden[q, g], downs, preferred_element_type=F32).astype(BF)
        value = value.reshape(2, slots, half)
        out[q, g], came[q, g] = value[0], send(value[1], core=1)

    def weigh(q, g):
        rows = jnp.concatenate([out[q, g], came[q, g]])
        return lax.dot_general(
            pays[g][order[q]], rows, (((0,), (0,)), ((), ())), preferred_element_type=F32
        )

    def before_weigh(q, value):
        came[q, 1], value = together((came[q, 1], value))
        return value

    def before_down(q, value):
        hidden[q, 1], value = together((hidden[q, 1], value))
        return value

    middle, back, forth = {}, {}, {}
    finish(0)
    hidden[0, 0], info_x = together((hidden[0, 0], info_x))
    down_product(0, 0)
    pays.append(places(info_x)[1])
    middle[0] = weigh(0, 0).astype(BF)
    middle[0], sent = together((middle[0], sent))
    part += [send(value, flip=2) for value in sent[2:]]
    middle[0] = send(middle[0], 1)
    down_product(0, 1)
    middle[0], part[1] = before_weigh(0, (middle[0], part[1]))
    middle[1] = send(weigh(0, 1).astype(BF), 1)
    finish(1)
    down_product(1, 0)
    back[0] = send(weigh(1, 0).astype(BF), -1)
    part[2] = before_down(1, part[2])
    down_product(1, 1)
    middle[1] = before_weigh(1, middle[1])
    back[1] = send(weigh(1, 1).astype(BF), -1)
    finish(2)
    down_product(2, 0)
    part[3] = before_down(2, part[3])
    down_product(2, 1)
    finish(3)
    down_product(3, 0)
    forth[0] = send((weigh(3, 0) + middle[0].astype(F32)).astype(BF), 1)
    hidden[3, 1] = before_weigh(2, hidden[3, 1])
    term = [weigh(2, g) for g in range(2)]
    down_product(3, 1)
    back = before_weigh(3, back)
    theirs = send((term[1] + back[1].astype(F32)).astype(BF), flip=1)
    forth[1] = send((weigh(3, 1) + middle[1].astype(F32)).astype(BF), 1, 1)
    mine = (term[0] + back[0].astype(F32) + forth[0].astype(F32)).astype(BF)
    far = (theirs.astype(F32) + forth[1].astype(F32)).astype(BF)

    mixed = jnp.zeros(tokens.shape, BF)
    for r, piece in enumerate(
        [mine[:, :quarter], far[:, :quarter], mine[:, quarter:], far[:, quarter:]]
    ):
        mixed = lax.dynamic_update_slice_in_dim(mixed, piece, (d ^ r) * quarter, axis=1)
    return mixed


def solution(mesh):
    placed = (
        P(("dp", "expert"), None),
        P("expert", "dp", None),
        P("expert", None, "dp"),
        P(("dp", "expert"), None),
        P(("dp", "expert"), None),
    )
    short = mesh.shape["expert"] == 8 and mesh.shape["dp"] == 4
    return jax.shard_map(
        paired if short else gathered,
        mesh=mesh,
        in_specs=placed,
        out_specs=P(("dp", "expert"), None),
        check_vma=False,
    )
```

```python
import jax
import jax.numpy as jnp
from jax import lax
from jax.sharding import PartitionSpec as P

BF = jnp.bfloat16
F32 = jnp.float32

def gathered(tokens, gate_up, down_proj, expert_ids, gate_weights):
    owners = lax.axis_size("expert")
    tok_rows = tokens.shape[0]
    width = tokens.shape[1]
    hidden_units = down_proj.shape[1]
    slots = 4 * tok_rows // owners
    total_rows = owners * slots
    owner_ids = jnp.arange(owners, dtype=jnp.int32)
    matches = expert_ids[:, :, None] == owner_ids[None, None, :]
    hits = jnp.sum(matches.astype(jnp.int32), axis=1)
    pick_weight = jnp.sum(
        jnp.where(matches, gate_weights[:, :, None].astype(F32), 0.0), axis=1
    )
    before = jnp.cumsum(hits, axis=0) - hits
    target = jnp.where(hits > 0, owner_ids[None, :] * slots + before, -1)
    slot_owner = jnp.arange(total_rows, dtype=jnp.int32) // slots
    slot_ids = jnp.arange(total_rows, dtype=jnp.int32)
    placed = jnp.take(target, slot_owner, axis=1) == slot_ids[None, :]
    place_bf = placed.astype(BF)
    outgoing = jnp.dot(place_bf.T, tokens, preferred_element_type=F32).astype(BF)
    arrived = lax.all_to_all(
        outgoing.reshape(owners, slots, width), "expert", split_axis=0, concat_axis=0, tiled=True
    )
    rows = arrived.reshape(total_rows, width)
    gu = jnp.dot(
        rows,
        lax.all_gather(gate_up, "dp", axis=1, tiled=True)[0],
        preferred_element_type=F32,
    )
    hidden = (jax.nn.silu(gu[:, :hidden_units]) * gu[:, hidden_units:]).astype(BF)
    result = jnp.dot(
        hidden,
        lax.all_gather(down_proj, "dp", axis=2, tiled=True)[0],
        preferred_element_type=F32,
    ).astype(BF)
    returned = lax.all_to_all(
        result.reshape(owners, slots, width), "expert", split_axis=0, concat_axis=0, tiled=True
    )
    weighted = (place_bf.astype(F32) * jnp.take(pick_weight, slot_owner, axis=1)).astype(BF)
    mixed = jnp.dot(weighted, returned.reshape(total_rows, width), preferred_element_type=F32)
    return mixed.astype(BF)


def paired(tokens, gate_up, down_proj, expert_ids, gate_weights):
    owners = lax.axis_size("expert")
    chips = owners // 2
    tok = tokens.shape[0]
    quarter = gate_up.shape[1]
    half = 2 * quarter
    ff = down_proj.shape[1]
    slots = 4 * tok // owners
    chunk = 2 * slots
    d = lax.axis_index("dp")
    e = lax.axis_index("expert")
    gate, down = gate_up[0], down_proj[0]
    together = lax.optimization_barrier

    def send(value, along=0, flip=0, core=0):
        return lax.ppermute(
            value,
            ("dp", "expert"),
            [
                (i * owners + j, (i ^ flip) * owners + ((j ^ core) + 2 * along) % owners)
                for i in range(4)
                for j in range(owners)
            ],
        )

    def depths(r):
        return lax.dynamic_slice_in_dim(tokens, (d ^ r) * quarter, quarter, axis=1)

    info = jnp.concatenate([expert_ids.T.astype(BF), gate_weights.T], axis=1)
    info = jnp.pad(info, ((0, 0), (0, half - 2 * tok)))

    def payload(r):
        return jnp.concatenate([jnp.concatenate([depths(r), depths(r + 1)], axis=1), info])

    first, second = payload(0), payload(2)
    gate_x = send(gate, flip=1)

    seen = [{0: first, 1: send(first, 1)}, {0: send(second, flip=2)}]
    seen[0][0], seen[1][0], down = together((seen[0][0], seen[1][0], down))
    down_y = send(down, flip=2)
    seen[1][1] = send(seen[1][0], 1)
    for held in seen:
        held[3] = send(held[0], -1)
        held[2] = send(held[1], 1)
    downs = jnp.concatenate([down, down_y], axis=1)
    seen[1][2], downs = together((seen[1][2], downs))

    chosen = jnp.stack([e, e ^ 1]).astype(jnp.int32)
    earlier = jnp.triu(jnp.ones((tok, tok), BF), 1)

    def places(info):
        matches = info[:, None, :, :tok].astype(jnp.int32) == chosen[:, None, None]
        hits = jnp.any(matches, axis=2)
        weight = jnp.sum(jnp.where(matches, info[:, None, :, tok:].astype(F32), 0.0), axis=2)
        rank = jnp.dot(hits.astype(BF), earlier, preferred_element_type=F32)
        rank = jnp.where(hits, rank, -1.0)
        place = (rank[..., None, :] == jnp.arange(slots, dtype=F32)[:, None]).astype(BF)
        pay = place * weight[..., None, :].astype(BF)
        return place, pay.reshape(chips, chunk, tok)

    infos = [jnp.stack([seen[g][k][tok:, : 2 * tok] for k in range(chips)]) for g in range(2)]
    helds = [jnp.stack([seen[g][k][:tok] for k in range(chips)]) for g in range(2)]
    info_x = send(infos[0], flip=1)
    place0, pay0 = places(infos[0])
    place1, _ = places(infos[1])

    def choose(place, held):
        def of(expert):
            return jnp.einsum(
                "zst,ztk->zsk", place[:, expert], held, preferred_element_type=F32
            ).astype(BF)

        other = send(of(1), core=1)
        return jnp.concatenate([of(0), other], axis=1)

    chosen0, chosen1 = choose(place0, helds[0]), choose(place1, helds[1])

    chosen1, gate_x = together((chosen1, gate_x))
    weights = jnp.concatenate([gate, gate_x])

    def product(rows):
        flat = rows.reshape(-1, half)
        return jnp.dot(flat, weights, preferred_element_type=F32).reshape(chips, chunk, 2 * ff)

    order = (2, 1, 0, 3)
    sent = product(chosen1).astype(BF)
    sent, chosen0 = together((sent, chosen0))
    sent = [sent[k] for k in order]
    part = [send(sent[0], flip=2)]
    near = product(chosen0)
    pays = [pay0]

    hidden, out, came = {}, {}, {}

    def finish(q):
        gu = near[order[q]] + part[q].astype(F32)
        own = (jax.nn.silu(gu[:, :ff]) * gu[:, ff:]).astype(BF)
        hidden[q, 0], hidden[q, 1] = own, send(own, flip=1)

    def down_product(q, g):
        value = jnp.dot(hidden[q, g], downs, preferred_element_type=F32).astype(BF)
        value = value.reshape(2, slots, half)
        out[q, g], came[q, g] = value[0], send(value[1], core=1)

    def weigh(q, g):
        rows = jnp.concatenate([out[q, g], came[q, g]])
        return lax.dot_general(
            pays[g][order[q]], rows, (((0,), (0,)), ((), ())), preferred_element_type=F32
        )

    def before_weigh(q, value):
        came[q, 1], value = together((came[q, 1], value))
        return value

    def before_down(q, value):
        hidden[q, 1], value = together((hidden[q, 1], value))
        return value

    middle, back, forth = {}, {}, {}
    finish(0)
    hidden[0, 0], info_x, sent = together((hidden[0, 0], info_x, sent))
    part.append(send(sent[1], flip=2))
    down_product(0, 0)
    pays.append(places(info_x)[1])
    middle[0] = weigh(0, 0).astype(BF)
    middle[0], sent = together((middle[0], sent))
    part += [send(value, flip=2) for value in sent[2:]]
    middle[0] = send(middle[0], 1)
    down_product(0, 1)
    middle[1], part[1] = together((weigh(0, 1).astype(BF), part[1]))
    middle[1] = send(middle[1], 1)
    middle[0], part[1] = together((middle[0], part[1]))
    finish(1)
    down_product(1, 0)
    came[1, 0], middle[1] = together((came[1, 0], middle[1]))
    back[0] = send(weigh(1, 0).astype(BF), -1)
    part[2] = before_down(1, part[2])
    down_product(1, 1)
    middle[1] = before_weigh(1, middle[1])
    back[1] = send(weigh(1, 1).astype(BF), -1)
    finish(2)
    down_product(2, 0)
    part[3] = before_down(2, part[3])
    down_product(2, 1)
    finish(3)
    down_product(3, 0)
    forth[0] = send((weigh(3, 0) + middle[0].astype(F32)).astype(BF), 1)
    hidden[3, 1] = before_weigh(2, hidden[3, 1])
    term = [weigh(2, g) for g in range(2)]
    down_product(3, 1)
    back = before_weigh(3, back)
    theirs = send((term[1] + back[1].astype(F32)).astype(BF), flip=1)
    forth[1] = send((weigh(3, 1) + middle[1].astype(F32)).astype(BF), 1, 1)
    mine = (term[0] + back[0].astype(F32) + forth[0].astype(F32)).astype(BF)
    far = (theirs.astype(F32) + forth[1].astype(F32)).astype(BF)

    mixed = jnp.zeros(tokens.shape, BF)
    for r, piece in enumerate(
        [mine[:, :quarter], far[:, :quarter], mine[:, quarter:], far[:, quarter:]]
    ):
        mixed = lax.dynamic_update_slice_in_dim(mixed, piece, (d ^ r) * quarter, axis=1)
    return mixed


def solution(mesh):
    placed = (
        P(("dp", "expert"), None),
        P("expert", "dp", None),
        P("expert", None, "dp"),
        P(("dp", "expert"), None),
        P(("dp", "expert"), None),
    )
    short = mesh.shape["expert"] == 8 and mesh.shape["dp"] == 4
    return jax.shard_map(
        paired if short else gathered,
        mesh=mesh,
        in_specs=placed,
        out_specs=P(("dp", "expert"), None),
        check_vma=False,
    )
```

```python
import jax
import jax.numpy as jnp
from jax import lax
from jax.sharding import PartitionSpec as P

BF = jnp.bfloat16
F32 = jnp.float32

def gathered(tokens, gate_up, down_proj, expert_ids, gate_weights):
    owners = lax.axis_size("expert")
    tok_rows = tokens.shape[0]
    width = tokens.shape[1]
    hidden_units = down_proj.shape[1]
    slots = 4 * tok_rows // owners
    total_rows = owners * slots
    owner_ids = jnp.arange(owners, dtype=jnp.int32)
    matches = expert_ids[:, :, None] == owner_ids[None, None, :]
    hits = jnp.sum(matches.astype(jnp.int32), axis=1)
    pick_weight = jnp.sum(
        jnp.where(matches, gate_weights[:, :, None].astype(F32), 0.0), axis=1
    )
    before = jnp.cumsum(hits, axis=0) - hits
    target = jnp.where(hits > 0, owner_ids[None, :] * slots + before, -1)
    slot_owner = jnp.arange(total_rows, dtype=jnp.int32) // slots
    slot_ids = jnp.arange(total_rows, dtype=jnp.int32)
    placed = jnp.take(target, slot_owner, axis=1) == slot_ids[None, :]
    place_bf = placed.astype(BF)
    outgoing = jnp.dot(place_bf.T, tokens, preferred_element_type=F32).astype(BF)
    arrived = lax.all_to_all(
        outgoing.reshape(owners, slots, width), "expert", split_axis=0, concat_axis=0, tiled=True
    )
    rows = arrived.reshape(total_rows, width)
    gu = jnp.dot(
        rows,
        lax.all_gather(gate_up, "dp", axis=1, tiled=True)[0],
        preferred_element_type=F32,
    )
    hidden = (jax.nn.silu(gu[:, :hidden_units]) * gu[:, hidden_units:]).astype(BF)
    result = jnp.dot(
        hidden,
        lax.all_gather(down_proj, "dp", axis=2, tiled=True)[0],
        preferred_element_type=F32,
    ).astype(BF)
    returned = lax.all_to_all(
        result.reshape(owners, slots, width), "expert", split_axis=0, concat_axis=0, tiled=True
    )
    weighted = (place_bf.astype(F32) * jnp.take(pick_weight, slot_owner, axis=1)).astype(BF)
    mixed = jnp.dot(weighted, returned.reshape(total_rows, width), preferred_element_type=F32)
    return mixed.astype(BF)


def paired(tokens, gate_up, down_proj, expert_ids, gate_weights):
    owners = lax.axis_size("expert")
    chips = owners // 2
    tok = tokens.shape[0]
    quarter = gate_up.shape[1]
    half = 2 * quarter
    ff = down_proj.shape[1]
    slots = 4 * tok // owners
    chunk = 2 * slots
    d = lax.axis_index("dp")
    e = lax.axis_index("expert")
    gate, down = gate_up[0], down_proj[0]
    together = lax.optimization_barrier

    def send(value, along=0, flip=0, core=0):
        return lax.ppermute(
            value,
            ("dp", "expert"),
            [
                (i * owners + j, (i ^ flip) * owners + ((j ^ core) + 2 * along) % owners)
                for i in range(4)
                for j in range(owners)
            ],
        )

    def depths(r):
        return lax.dynamic_slice_in_dim(tokens, (d ^ r) * quarter, quarter, axis=1)

    info = jnp.concatenate([expert_ids.T.astype(BF), gate_weights.T], axis=1)
    info = jnp.pad(info, ((0, 0), (0, half - 2 * tok)))

    def payload(r):
        return jnp.concatenate([jnp.concatenate([depths(r), depths(r + 1)], axis=1), info])

    first, second = payload(0), payload(2)
    gate_x = send(gate, flip=1)

    seen = [{0: first, 1: send(first, 1)}, {0: send(second, flip=2)}]
    seen[0][0], seen[1][0], down = together((seen[0][0], seen[1][0], down))
    down_y = send(down, flip=2)
    seen[1][1] = send(seen[1][0], 1)
    for held in seen:
        held[3] = send(held[0], -1)
        held[2] = send(held[1], 1)
    downs = jnp.concatenate([down, down_y], axis=1)
    seen[1][2], downs = together((seen[1][2], downs))

    chosen = jnp.stack([e, e ^ 1]).astype(jnp.int32)
    earlier = jnp.triu(jnp.ones((tok, tok), BF), 1)

    def places(info):
        matches = info[:, None, :, :tok].astype(jnp.int32) == chosen[:, None, None]
        hits = jnp.any(matches, axis=2)
        weight = jnp.sum(jnp.where(matches, info[:, None, :, tok:].astype(F32), 0.0), axis=2)
        rank = jnp.dot(hits.astype(BF), earlier, preferred_element_type=F32)
        rank = jnp.where(hits, rank, -1.0)
        place = (rank[..., None, :] == jnp.arange(slots, dtype=F32)[:, None]).astype(BF)
        pay = place * weight[..., None, :].astype(BF)
        return place, pay.reshape(chips, chunk, tok)

    infos = [jnp.stack([seen[g][k][tok:, : 2 * tok] for k in range(chips)]) for g in range(2)]
    helds = [jnp.stack([seen[g][k][:tok] for k in range(chips)]) for g in range(2)]
    info_x = send(infos[0], flip=1)
    place0, pay0 = places(infos[0])
    place1, _ = places(infos[1])

    def choose(place, held):
        def of(expert):
            return jnp.einsum(
                "zst,ztk->zsk", place[:, expert], held, preferred_element_type=F32
            ).astype(BF)

        other = send(of(1), core=1)
        return jnp.concatenate([of(0), other], axis=1)

    chosen0, chosen1 = choose(place0, helds[0]), choose(place1, helds[1])

    chosen1, gate_x = together((chosen1, gate_x))
    weights = jnp.concatenate([gate, gate_x])

    def product(rows, lo=0, hi=2 * ff):
        flat = rows.reshape(-1, half)
        return jnp.dot(flat, weights[:, lo:hi], preferred_element_type=F32).reshape(
            chips, chunk, hi - lo
        )

    order = (2, 1, 0, 3)
    gates = product(chosen1, 0, ff).astype(BF)
    gates, chosen1 = together((gates, chosen1))
    gate_part = send(gates[order[0]], flip=2)
    ups = product(chosen1, ff).astype(BF)
    ups, chosen0 = together((ups, chosen0))
    part = [send(ups[order[0]], flip=2)]
    chosen0, gate_part = together((chosen0, gate_part))
    part[0] = jnp.concatenate([gate_part, part[0]], axis=1)
    near = product(chosen0)
    pays = [pay0]

    hidden, out, came = {}, {}, {}

    def finish(q):
        gu = near[order[q]] + part[q].astype(F32)
        own = (jax.nn.silu(gu[:, :ff]) * gu[:, ff:]).astype(BF)
        hidden[q, 0], hidden[q, 1] = own, send(own, flip=1)

    def down_product(q, g):
        value = jnp.dot(hidden[q, g], downs, preferred_element_type=F32).astype(BF)
        value = value.reshape(2, slots, half)
        out[q, g], came[q, g] = value[0], send(value[1], core=1)

    def weigh(q, g):
        rows = jnp.concatenate([out[q, g], came[q, g]])
        return lax.dot_general(
            pays[g][order[q]], rows, (((0,), (0,)), ((), ())), preferred_element_type=F32
        )

    def before_weigh(q, value):
        came[q, 1], value = together((came[q, 1], value))
        return value

    def before_down(q, value):
        hidden[q, 1], value = together((hidden[q, 1], value))
        return value

    middle, back, forth = {}, {}, {}
    finish(0)
    hidden[0, 0], info_x = together((hidden[0, 0], info_x))
    down_product(0, 0)
    out[0, 0], gates, ups = together((out[0, 0], gates, ups))

    def whole(q):
        return jnp.concatenate([gates[order[q]], ups[order[q]]], axis=1)

    part.append(send(whole(1), flip=2))
    pays.append(places(info_x)[1])
    middle[0] = weigh(0, 0).astype(BF)
    middle[0], gates, ups = together((middle[0], gates, ups))
    part += [send(whole(q), flip=2) for q in range(2, chips)]
    middle[0] = send(middle[0], 1)
    down_product(0, 1)
    middle[0], part[1] = before_weigh(0, (middle[0], part[1]))
    middle[1] = send(weigh(0, 1).astype(BF), 1)
    finish(1)
    down_product(1, 0)
    back[0] = send(weigh(1, 0).astype(BF), -1)
    part[2] = before_down(1, part[2])
    down_product(1, 1)
    middle[1] = before_weigh(1, middle[1])
    back[1] = send(weigh(1, 1).astype(BF), -1)
    finish(2)
    down_product(2, 0)
    part[3] = before_down(2, part[3])
    down_product(2, 1)
    finish(3)
    down_product(3, 0)
    forth[0] = send((weigh(3, 0) + middle[0].astype(F32)).astype(BF), 1)
    hidden[3, 1] = before_weigh(2, hidden[3, 1])
    term = [weigh(2, g) for g in range(2)]
    down_product(3, 1)
    back = before_weigh(3, back)
    theirs = send((term[1] + back[1].astype(F32)).astype(BF), flip=1)
    forth[1] = send((weigh(3, 1) + middle[1].astype(F32)).astype(BF), 1, 1)
    mine = (term[0] + back[0].astype(F32) + forth[0].astype(F32)).astype(BF)
    far = (theirs.astype(F32) + forth[1].astype(F32)).astype(BF)

    mixed = jnp.zeros(tokens.shape, BF)
    for r, piece in enumerate(
        [mine[:, :quarter], far[:, :quarter], mine[:, quarter:], far[:, quarter:]]
    ):
        mixed = lax.dynamic_update_slice_in_dim(mixed, piece, (d ^ r) * quarter, axis=1)
    return mixed


def solution(mesh):
    placed = (
        P(("dp", "expert"), None),
        P("expert", "dp", None),
        P("expert", None, "dp"),
        P(("dp", "expert"), None),
        P(("dp", "expert"), None),
    )
    short = mesh.shape["expert"] == 8 and mesh.shape["dp"] == 4
    return jax.shard_map(
        paired if short else gathered,
        mesh=mesh,
        in_specs=placed,
        out_specs=P(("dp", "expert"), None),
        check_vma=False,
    )
```

```python
import jax
import jax.numpy as jnp
from jax import lax
from jax.sharding import PartitionSpec as P

BF = jnp.bfloat16
F32 = jnp.float32

def gathered(tokens, gate_up, down_proj, expert_ids, gate_weights):
    owners = lax.axis_size("expert")
    tok_rows = tokens.shape[0]
    width = tokens.shape[1]
    hidden_units = down_proj.shape[1]
    slots = 4 * tok_rows // owners
    total_rows = owners * slots
    owner_ids = jnp.arange(owners, dtype=jnp.int32)
    matches = expert_ids[:, :, None] == owner_ids[None, None, :]
    hits = jnp.sum(matches.astype(jnp.int32), axis=1)
    pick_weight = jnp.sum(
        jnp.where(matches, gate_weights[:, :, None].astype(F32), 0.0), axis=1
    )
    before = jnp.cumsum(hits, axis=0) - hits
    target = jnp.where(hits > 0, owner_ids[None, :] * slots + before, -1)
    slot_owner = jnp.arange(total_rows, dtype=jnp.int32) // slots
    slot_ids = jnp.arange(total_rows, dtype=jnp.int32)
    placed = jnp.take(target, slot_owner, axis=1) == slot_ids[None, :]
    place_bf = placed.astype(BF)
    outgoing = jnp.dot(place_bf.T, tokens, preferred_element_type=F32).astype(BF)
    arrived = lax.all_to_all(
        outgoing.reshape(owners, slots, width), "expert", split_axis=0, concat_axis=0, tiled=True
    )
    rows = arrived.reshape(total_rows, width)
    gu = jnp.dot(
        rows,
        lax.all_gather(gate_up, "dp", axis=1, tiled=True)[0],
        preferred_element_type=F32,
    )
    hidden = (jax.nn.silu(gu[:, :hidden_units]) * gu[:, hidden_units:]).astype(BF)
    result = jnp.dot(
        hidden,
        lax.all_gather(down_proj, "dp", axis=2, tiled=True)[0],
        preferred_element_type=F32,
    ).astype(BF)
    returned = lax.all_to_all(
        result.reshape(owners, slots, width), "expert", split_axis=0, concat_axis=0, tiled=True
    )
    weighted = (place_bf.astype(F32) * jnp.take(pick_weight, slot_owner, axis=1)).astype(BF)
    mixed = jnp.dot(weighted, returned.reshape(total_rows, width), preferred_element_type=F32)
    return mixed.astype(BF)


def paired(tokens, gate_up, down_proj, expert_ids, gate_weights):
    owners = lax.axis_size("expert")
    chips = owners // 2
    tok = tokens.shape[0]
    quarter = gate_up.shape[1]
    half = 2 * quarter
    ff = down_proj.shape[1]
    slots = 4 * tok // owners
    chunk = 2 * slots
    d = lax.axis_index("dp")
    e = lax.axis_index("expert")
    gate, down = gate_up[0], down_proj[0]
    together = lax.optimization_barrier

    def send(value, along=0, flip=0, core=0):
        return lax.ppermute(
            value,
            ("dp", "expert"),
            [
                (i * owners + j, (i ^ flip) * owners + ((j ^ core) + 2 * along) % owners)
                for i in range(4)
                for j in range(owners)
            ],
        )

    def depths(r):
        return lax.dynamic_slice_in_dim(tokens, (d ^ r) * quarter, quarter, axis=1)

    info = jnp.concatenate([expert_ids.T.astype(BF), gate_weights.T], axis=1)
    info = jnp.pad(info, ((0, 0), (0, half - 2 * tok)))

    def payload(r):
        return jnp.concatenate([jnp.concatenate([depths(r), depths(r + 1)], axis=1), info])

    first, second = payload(0), payload(2)
    gate_x = send(gate, flip=1)

    seen = [{0: first, 1: send(first, 1)}, {0: send(second, flip=2)}]
    seen[0][0], seen[1][0], down = together((seen[0][0], seen[1][0], down))
    down_y = send(down, flip=2)
    seen[1][1] = send(seen[1][0], 1)
    for held in seen:
        held[3] = send(held[0], -1)
        held[2] = send(held[1], 1)
    downs = jnp.concatenate([down, down_y], axis=1)
    seen[1][2], downs = together((seen[1][2], downs))

    chosen = jnp.stack([e, e ^ 1]).astype(jnp.int32)
    earlier = jnp.triu(jnp.ones((tok, tok), BF), 1)

    def places(info):
        matches = info[:, None, :, :tok].astype(jnp.int32) == chosen[:, None, None]
        hits = jnp.any(matches, axis=2)
        weight = jnp.sum(jnp.where(matches, info[:, None, :, tok:].astype(F32), 0.0), axis=2)
        rank = jnp.dot(hits.astype(BF), earlier, preferred_element_type=F32)
        rank = jnp.where(hits, rank, -1.0)
        place = (rank[..., None, :] == jnp.arange(slots, dtype=F32)[:, None]).astype(BF)
        pay = place * weight[..., None, :].astype(BF)
        return place, pay.reshape(chips, chunk, tok)

    infos = [jnp.stack([seen[g][k][tok:, : 2 * tok] for k in range(chips)]) for g in range(2)]
    helds = [jnp.stack([seen[g][k][:tok] for k in range(chips)]) for g in range(2)]
    info_x = send(infos[0], flip=1)
    place0, pay0 = places(infos[0])
    place1, _ = places(infos[1])

    def choose(place, held):
        def of(expert):
            return jnp.einsum(
                "zst,ztk->zsk", place[:, expert], held, preferred_element_type=F32
            ).astype(BF)

        other = send(of(1), core=1)
        return jnp.concatenate([of(0), other], axis=1)

    chosen0, chosen1 = choose(place0, helds[0]), choose(place1, helds[1])

    chosen1, gate_x = together((chosen1, gate_x))
    weights = jnp.concatenate([gate, gate_x])

    def product(rows, lo=0, hi=2 * ff):
        flat = rows.reshape(-1, half)
        return jnp.dot(flat, weights[:, lo:hi], preferred_element_type=F32).reshape(
            chips, chunk, hi - lo
        )

    order = (2, 1, 0, 3)
    gates = product(chosen1, 0, ff).astype(BF)
    gates, chosen1 = together((gates, chosen1))
    gate_part = send(gates[order[0]], flip=2)
    ups = product(chosen1, ff).astype(BF)
    ups, chosen0 = together((ups, chosen0))
    part = [send(ups[order[0]], flip=2)]
    chosen0, gate_part = together((chosen0, gate_part))
    part[0] = jnp.concatenate([gate_part, part[0]], axis=1)
    near = product(chosen0)
    pays = [pay0]

    hidden, out, came = {}, {}, {}

    def finish(q):
        gu = near[order[q]] + part[q].astype(F32)
        own = (jax.nn.silu(gu[:, :ff]) * gu[:, ff:]).astype(BF)
        hidden[q, 0], hidden[q, 1] = own, send(own, flip=1)

    def down_product(q, g):
        value = jnp.dot(hidden[q, g], downs, preferred_element_type=F32).astype(BF)
        value = value.reshape(2, slots, half)
        out[q, g], came[q, g] = value[0], send(value[1], core=1)

    def weigh(q, g):
        rows = jnp.concatenate([out[q, g], came[q, g]])
        return lax.dot_general(
            pays[g][order[q]], rows, (((0,), (0,)), ((), ())), preferred_element_type=F32
        )

    def before_weigh(q, value):
        came[q, 1], value = together((came[q, 1], value))
        return value

    def before_down(q, value):
        hidden[q, 1], value = together((hidden[q, 1], value))
        return value

    middle, back, forth = {}, {}, {}
    finish(0)
    hidden[0, 0], info_x = together((hidden[0, 0], info_x))
    down_product(0, 0)
    pays.append(places(info_x)[1])
    middle[0] = weigh(0, 0).astype(BF)
    hidden[0, 1], gates, ups = together((hidden[0, 1], gates, ups))
    part += [
        send(jnp.concatenate([gates[order[q]], ups[order[q]]], axis=1), flip=2)
        for q in range(1, chips)
    ]
    middle[0] = send(middle[0], 1)
    down_product(0, 1)
    middle[0], part[1] = before_weigh(0, (middle[0], part[1]))
    middle[1] = send(weigh(0, 1).astype(BF), 1)
    finish(1)
    down_product(1, 0)
    back[0] = send(weigh(1, 0).astype(BF), -1)
    part[2] = before_down(1, part[2])
    down_product(1, 1)
    middle[1] = before_weigh(1, middle[1])
    back[1] = send(weigh(1, 1).astype(BF), -1)
    finish(2)
    down_product(2, 0)
    part[3] = before_down(2, part[3])
    down_product(2, 1)
    finish(3)
    down_product(3, 0)
    forth[0] = send((weigh(3, 0) + middle[0].astype(F32)).astype(BF), 1)
    hidden[3, 1] = before_weigh(2, hidden[3, 1])
    term = [weigh(2, g) for g in range(2)]
    down_product(3, 1)
    back = before_weigh(3, back)
    theirs = send((term[1] + back[1].astype(F32)).astype(BF), flip=1)
    forth[1] = send((weigh(3, 1) + middle[1].astype(F32)).astype(BF), 1, 1)
    mine = (term[0] + back[0].astype(F32) + forth[0].astype(F32)).astype(BF)
    far = (theirs.astype(F32) + forth[1].astype(F32)).astype(BF)

    mixed = jnp.zeros(tokens.shape, BF)
    for r, piece in enumerate(
        [mine[:, :quarter], far[:, :quarter], mine[:, quarter:], far[:, quarter:]]
    ):
        mixed = lax.dynamic_update_slice_in_dim(mixed, piece, (d ^ r) * quarter, axis=1)
    return mixed


def solution(mesh):
    placed = (
        P(("dp", "expert"), None),
        P("expert", "dp", None),
        P("expert", None, "dp"),
        P(("dp", "expert"), None),
        P(("dp", "expert"), None),
    )
    short = mesh.shape["expert"] == 8 and mesh.shape["dp"] == 4
    return jax.shard_map(
        paired if short else gathered,
        mesh=mesh,
        in_specs=placed,
        out_specs=P(("dp", "expert"), None),
        check_vma=False,
    )
```

```python
import jax
import jax.numpy as jnp
from jax import lax
from jax.sharding import PartitionSpec as P

BF = jnp.bfloat16
F32 = jnp.float32

def gathered(tokens, gate_up, down_proj, expert_ids, gate_weights):
    owners = lax.axis_size("expert")
    tok_rows = tokens.shape[0]
    width = tokens.shape[1]
    hidden_units = down_proj.shape[1]
    slots = 4 * tok_rows // owners
    total_rows = owners * slots
    owner_ids = jnp.arange(owners, dtype=jnp.int32)
    matches = expert_ids[:, :, None] == owner_ids[None, None, :]
    hits = jnp.sum(matches.astype(jnp.int32), axis=1)
    pick_weight = jnp.sum(
        jnp.where(matches, gate_weights[:, :, None].astype(F32), 0.0), axis=1
    )
    before = jnp.cumsum(hits, axis=0) - hits
    target = jnp.where(hits > 0, owner_ids[None, :] * slots + before, -1)
    slot_owner = jnp.arange(total_rows, dtype=jnp.int32) // slots
    slot_ids = jnp.arange(total_rows, dtype=jnp.int32)
    placed = jnp.take(target, slot_owner, axis=1) == slot_ids[None, :]
    place_bf = placed.astype(BF)
    outgoing = jnp.dot(place_bf.T, tokens, preferred_element_type=F32).astype(BF)
    arrived = lax.all_to_all(
        outgoing.reshape(owners, slots, width), "expert", split_axis=0, concat_axis=0, tiled=True
    )
    rows = arrived.reshape(total_rows, width)
    gu = jnp.dot(
        rows,
        lax.all_gather(gate_up, "dp", axis=1, tiled=True)[0],
        preferred_element_type=F32,
    )
    hidden = (jax.nn.silu(gu[:, :hidden_units]) * gu[:, hidden_units:]).astype(BF)
    result = jnp.dot(
        hidden,
        lax.all_gather(down_proj, "dp", axis=2, tiled=True)[0],
        preferred_element_type=F32,
    ).astype(BF)
    returned = lax.all_to_all(
        result.reshape(owners, slots, width), "expert", split_axis=0, concat_axis=0, tiled=True
    )
    weighted = (place_bf.astype(F32) * jnp.take(pick_weight, slot_owner, axis=1)).astype(BF)
    mixed = jnp.dot(weighted, returned.reshape(total_rows, width), preferred_element_type=F32)
    return mixed.astype(BF)


def paired(tokens, gate_up, down_proj, expert_ids, gate_weights):
    owners = lax.axis_size("expert")
    chips = owners // 2
    tok = tokens.shape[0]
    quarter = gate_up.shape[1]
    half = 2 * quarter
    ff = down_proj.shape[1]
    slots = 4 * tok // owners
    chunk = 2 * slots
    d = lax.axis_index("dp")
    e = lax.axis_index("expert")
    gate, down = gate_up[0], down_proj[0]
    together = lax.optimization_barrier

    def send(value, along=0, flip=0, core=0):
        return lax.ppermute(
            value,
            ("dp", "expert"),
            [
                (i * owners + j, (i ^ flip) * owners + ((j ^ core) + 2 * along) % owners)
                for i in range(4)
                for j in range(owners)
            ],
        )

    def depths(r):
        return lax.dynamic_slice_in_dim(tokens, (d ^ r) * quarter, quarter, axis=1)

    info = jnp.concatenate([expert_ids.T.astype(BF), gate_weights.T], axis=1)
    info = jnp.pad(info, ((0, 0), (0, half - 2 * tok)))

    def payload(r):
        return jnp.concatenate([jnp.concatenate([depths(r), depths(r + 1)], axis=1), info])

    first, second = payload(0), payload(2)
    gate_x = send(gate, flip=1)

    seen = [{0: first, 1: send(first, 1)}, {0: send(second, flip=2)}]
    seen[0][0], seen[1][0], down = together((seen[0][0], seen[1][0], down))
    down_y = send(down, flip=2)
    seen[1][1] = send(seen[1][0], 1)
    for held in seen:
        held[3] = send(held[0], -1)
        held[2] = send(held[1], 1)
    downs = jnp.concatenate([down, down_y], axis=1)
    seen[1][2], downs = together((seen[1][2], downs))

    chosen = jnp.stack([e, e ^ 1]).astype(jnp.int32)
    earlier = jnp.triu(jnp.ones((tok, tok), BF), 1)

    def places(info):
        matches = info[:, None, :, :tok].astype(jnp.int32) == chosen[:, None, None]
        hits = jnp.any(matches, axis=2)
        weight = jnp.sum(jnp.where(matches, info[:, None, :, tok:].astype(F32), 0.0), axis=2)
        rank = jnp.dot(hits.astype(BF), earlier, preferred_element_type=F32)
        rank = jnp.where(hits, rank, -1.0)
        place = (rank[..., None, :] == jnp.arange(slots, dtype=F32)[:, None]).astype(BF)
        pay = place * weight[..., None, :].astype(BF)
        return place, pay.reshape(chips, chunk, tok)

    infos = [jnp.stack([seen[g][k][tok:, : 2 * tok] for k in range(chips)]) for g in range(2)]
    helds = [jnp.stack([seen[g][k][:tok] for k in range(chips)]) for g in range(2)]
    info_x = send(infos[0], flip=1)
    place0, pay0 = places(infos[0])
    place1, _ = places(infos[1])

    def choose(place, held):
        def of(expert):
            return jnp.einsum(
                "zst,ztk->zsk", place[:, expert], held, preferred_element_type=F32
            ).astype(BF)

        other = send(of(1), core=1)
        return jnp.concatenate([of(0), other], axis=1)

    chosen0, chosen1 = choose(place0, helds[0]), choose(place1, helds[1])

    chosen1, gate_x = together((chosen1, gate_x))
    weights = jnp.concatenate([gate, gate_x])

    def product(rows, lo=0, hi=2 * ff):
        flat = rows.reshape(-1, half)
        return jnp.dot(flat, weights[:, lo:hi], preferred_element_type=F32).reshape(
            chips, chunk, hi - lo
        )

    order = (2, 1, 0, 3)
    gates = product(chosen1, 0, ff).astype(BF)
    gates, chosen1 = together((gates, chosen1))
    gate_part = send(gates[order[0]], flip=2)
    ups = product(chosen1, ff).astype(BF)
    ups, chosen0 = together((ups, chosen0))
    part = [send(ups[order[0]], flip=2)]
    chosen0, gate_part = together((chosen0, gate_part))
    part[0] = jnp.concatenate([gate_part, part[0]], axis=1)
    near = product(chosen0)
    pays = [pay0]

    hidden, out, came = {}, {}, {}

    def finish(q):
        gu = near[order[q]] + part[q].astype(F32)
        own = (jax.nn.silu(gu[:, :ff]) * gu[:, ff:]).astype(BF)
        hidden[q, 0], hidden[q, 1] = own, send(own, flip=1)

    def down_product(q, g):
        value = jnp.dot(hidden[q, g], downs, preferred_element_type=F32).astype(BF)
        value = value.reshape(2, slots, half)
        out[q, g], came[q, g] = value[0], send(value[1], core=1)

    def weigh(q, g):
        rows = jnp.concatenate([out[q, g], came[q, g]])
        return lax.dot_general(
            pays[g][order[q]], rows, (((0,), (0,)), ((), ())), preferred_element_type=F32
        )

    def before_weigh(q, value):
        came[q, 1], value = together((came[q, 1], value))
        return value

    def before_down(q, value):
        hidden[q, 1], value = together((hidden[q, 1], value))
        return value

    middle, back, forth = {}, {}, {}
    finish(0)
    hidden[0, 0], info_x = together((hidden[0, 0], info_x))
    down_product(0, 0)
    pays.append(places(info_x)[1])
    middle[0] = weigh(0, 0).astype(BF)
    hidden[0, 1], gates, ups = together((hidden[0, 1], gates, ups))

    def whole(q):
        return jnp.concatenate([gates[order[q]], ups[order[q]]], axis=1)

    part.append(send(whole(1), flip=2))
    middle[0] = send(middle[0], 1)
    down_product(0, 1)
    middle[0], part[1] = before_weigh(0, (middle[0], part[1]))
    middle[0], gates, ups = together((middle[0], gates, ups))
    part += [send(whole(q), flip=2) for q in range(2, chips)]
    middle[1] = send(weigh(0, 1).astype(BF), 1)
    finish(1)
    down_product(1, 0)
    back[0] = send(weigh(1, 0).astype(BF), -1)
    part[2] = before_down(1, part[2])
    down_product(1, 1)
    middle[1] = before_weigh(1, middle[1])
    back[1] = send(weigh(1, 1).astype(BF), -1)
    finish(2)
    down_product(2, 0)
    part[3] = before_down(2, part[3])
    down_product(2, 1)
    finish(3)
    down_product(3, 0)
    forth[0] = send((weigh(3, 0) + middle[0].astype(F32)).astype(BF), 1)
    hidden[3, 1] = before_weigh(2, hidden[3, 1])
    term = [weigh(2, g) for g in range(2)]
    down_product(3, 1)
    back = before_weigh(3, back)
    theirs = send((term[1] + back[1].astype(F32)).astype(BF), flip=1)
    forth[1] = send((weigh(3, 1) + middle[1].astype(F32)).astype(BF), 1, 1)
    mine = (term[0] + back[0].astype(F32) + forth[0].astype(F32)).astype(BF)
    far = (theirs.astype(F32) + forth[1].astype(F32)).astype(BF)

    mixed = jnp.zeros(tokens.shape, BF)
    for r, piece in enumerate(
        [mine[:, :quarter], far[:, :quarter], mine[:, quarter:], far[:, quarter:]]
    ):
        mixed = lax.dynamic_update_slice_in_dim(mixed, piece, (d ^ r) * quarter, axis=1)
    return mixed


def solution(mesh):
    placed = (
        P(("dp", "expert"), None),
        P("expert", "dp", None),
        P("expert", None, "dp"),
        P(("dp", "expert"), None),
        P(("dp", "expert"), None),
    )
    short = mesh.shape["expert"] == 8 and mesh.shape["dp"] == 4
    return jax.shard_map(
        paired if short else gathered,
        mesh=mesh,
        in_specs=placed,
        out_specs=P(("dp", "expert"), None),
        check_vma=False,
    )
```

```python
import jax
import jax.numpy as jnp
from jax import lax
from jax.sharding import PartitionSpec as P

BF = jnp.bfloat16
F32 = jnp.float32

def gathered(tokens, gate_up, down_proj, expert_ids, gate_weights):
    owners = lax.axis_size("expert")
    tok_rows = tokens.shape[0]
    width = tokens.shape[1]
    hidden_units = down_proj.shape[1]
    slots = 4 * tok_rows // owners
    total_rows = owners * slots
    owner_ids = jnp.arange(owners, dtype=jnp.int32)
    matches = expert_ids[:, :, None] == owner_ids[None, None, :]
    hits = jnp.sum(matches.astype(jnp.int32), axis=1)
    pick_weight = jnp.sum(
        jnp.where(matches, gate_weights[:, :, None].astype(F32), 0.0), axis=1
    )
    before = jnp.cumsum(hits, axis=0) - hits
    target = jnp.where(hits > 0, owner_ids[None, :] * slots + before, -1)
    slot_owner = jnp.arange(total_rows, dtype=jnp.int32) // slots
    slot_ids = jnp.arange(total_rows, dtype=jnp.int32)
    placed = jnp.take(target, slot_owner, axis=1) == slot_ids[None, :]
    place_bf = placed.astype(BF)
    outgoing = jnp.dot(place_bf.T, tokens, preferred_element_type=F32).astype(BF)
    arrived = lax.all_to_all(
        outgoing.reshape(owners, slots, width), "expert", split_axis=0, concat_axis=0, tiled=True
    )
    rows = arrived.reshape(total_rows, width)
    gu = jnp.dot(
        rows,
        lax.all_gather(gate_up, "dp", axis=1, tiled=True)[0],
        preferred_element_type=F32,
    )
    hidden = (jax.nn.silu(gu[:, :hidden_units]) * gu[:, hidden_units:]).astype(BF)
    result = jnp.dot(
        hidden,
        lax.all_gather(down_proj, "dp", axis=2, tiled=True)[0],
        preferred_element_type=F32,
    ).astype(BF)
    returned = lax.all_to_all(
        result.reshape(owners, slots, width), "expert", split_axis=0, concat_axis=0, tiled=True
    )
    weighted = (place_bf.astype(F32) * jnp.take(pick_weight, slot_owner, axis=1)).astype(BF)
    mixed = jnp.dot(weighted, returned.reshape(total_rows, width), preferred_element_type=F32)
    return mixed.astype(BF)


def paired(tokens, gate_up, down_proj, expert_ids, gate_weights):
    owners = lax.axis_size("expert")
    chips = owners // 2
    tok = tokens.shape[0]
    quarter = gate_up.shape[1]
    half = 2 * quarter
    ff = down_proj.shape[1]
    slots = 4 * tok // owners
    chunk = 2 * slots
    d = lax.axis_index("dp")
    e = lax.axis_index("expert")
    gate, down = gate_up[0], down_proj[0]
    together = lax.optimization_barrier

    def send(value, along=0, flip=0, core=0):
        return lax.ppermute(
            value,
            ("dp", "expert"),
            [
                (i * owners + j, (i ^ flip) * owners + ((j ^ core) + 2 * along) % owners)
                for i in range(4)
                for j in range(owners)
            ],
        )

    def depths(r):
        return lax.dynamic_slice_in_dim(tokens, (d ^ r) * quarter, quarter, axis=1)

    info = jnp.concatenate([expert_ids.T.astype(BF), gate_weights.T], axis=1)
    info = jnp.pad(info, ((0, 0), (0, half - 2 * tok)))

    def payload(r):
        return jnp.concatenate([jnp.concatenate([depths(r), depths(r + 1)], axis=1), info])

    first, second = payload(0), payload(2)
    gate_x = send(gate, flip=1)

    seen = [{0: first, 1: send(first, 1)}, {0: send(second, flip=2)}]
    seen[0][0], seen[1][0], down = together((seen[0][0], seen[1][0], down))
    down_y = send(down, flip=2)
    seen[1][1] = send(seen[1][0], 1)
    for held in seen:
        held[3] = send(held[0], -1)
        held[2] = send(held[1], 1)
    downs = jnp.concatenate([down, down_y], axis=1)
    seen[1][2], downs = together((seen[1][2], downs))

    chosen = jnp.stack([e, e ^ 1]).astype(jnp.int32)
    earlier = jnp.triu(jnp.ones((tok, tok), BF), 1)

    def places(info):
        matches = info[:, None, :, :tok].astype(jnp.int32) == chosen[:, None, None]
        hits = jnp.any(matches, axis=2)
        weight = jnp.sum(jnp.where(matches, info[:, None, :, tok:].astype(F32), 0.0), axis=2)
        rank = jnp.dot(hits.astype(BF), earlier, preferred_element_type=F32)
        rank = jnp.where(hits, rank, -1.0)
        place = (rank[..., None, :] == jnp.arange(slots, dtype=F32)[:, None]).astype(BF)
        pay = place * weight[..., None, :].astype(BF)
        return place, pay.reshape(chips, chunk, tok)

    infos = [jnp.stack([seen[g][k][tok:, : 2 * tok] for k in range(chips)]) for g in range(2)]
    helds = [jnp.stack([seen[g][k][:tok] for k in range(chips)]) for g in range(2)]
    info_x = send(infos[0], flip=1)
    place0, pay0 = places(infos[0])
    place1, _ = places(infos[1])

    def choose(place, held):
        def of(expert):
            return jnp.einsum(
                "zst,ztk->zsk", place[:, expert], held, preferred_element_type=F32
            ).astype(BF)

        other = send(of(1), core=1)
        return jnp.concatenate([of(0), other], axis=1)

    chosen0, chosen1 = choose(place0, helds[0]), choose(place1, helds[1])

    chosen1, gate_x = together((chosen1, gate_x))
    weights = jnp.concatenate([gate, gate_x])

    def product(rows, lo=0, hi=2 * ff):
        flat = rows.reshape(-1, half)
        return jnp.dot(flat, weights[:, lo:hi], preferred_element_type=F32).reshape(
            chips, chunk, hi - lo
        )

    order = (2, 1, 0, 3)
    gates = product(chosen1, 0, ff).astype(BF)
    gates, chosen1 = together((gates, chosen1))
    gate_part = send(gates[order[0]], flip=2)
    ups = product(chosen1, ff).astype(BF)
    ups, chosen0 = together((ups, chosen0))
    part = [send(ups[order[0]], flip=2)]
    chosen0, gate_part, gates, ups = together((chosen0, gate_part, gates, ups))
    part[0] = jnp.concatenate([gate_part, part[0]], axis=1)

    def whole(q):
        return jnp.concatenate([gates[order[q]], ups[order[q]]], axis=1)

    second = whole(1)
    chosen0, second = together((chosen0, second))
    part.append(send(second, flip=2))
    near = product(chosen0)
    pays = [pay0]

    hidden, out, came = {}, {}, {}

    def finish(q):
        gu = near[order[q]] + part[q].astype(F32)
        own = (jax.nn.silu(gu[:, :ff]) * gu[:, ff:]).astype(BF)
        hidden[q, 0], hidden[q, 1] = own, send(own, flip=1)

    def down_product(q, g):
        value = jnp.dot(hidden[q, g], downs, preferred_element_type=F32).astype(BF)
        value = value.reshape(2, slots, half)
        out[q, g], came[q, g] = value[0], send(value[1], core=1)

    def weigh(q, g):
        rows = jnp.concatenate([out[q, g], came[q, g]])
        return lax.dot_general(
            pays[g][order[q]], rows, (((0,), (0,)), ((), ())), preferred_element_type=F32
        )

    def before_weigh(q, value):
        came[q, 1], value = together((came[q, 1], value))
        return value

    def before_down(q, value):
        hidden[q, 1], value = together((hidden[q, 1], value))
        return value

    middle, back, forth = {}, {}, {}
    finish(0)
    hidden[0, 0], info_x = together((hidden[0, 0], info_x))
    down_product(0, 0)
    pays.append(places(info_x)[1])
    middle[0] = weigh(0, 0).astype(BF)
    middle[0], gates, ups = together((middle[0], gates, ups))
    part += [send(whole(q), flip=2) for q in range(2, chips)]
    middle[0] = send(middle[0], 1)
    part[1] = before_down(0, part[1])
    down_product(0, 1)
    middle[0] = before_weigh(0, middle[0])
    middle[1] = send(weigh(0, 1).astype(BF), 1)
    finish(1)
    down_product(1, 0)
    back[0] = send(weigh(1, 0).astype(BF), -1)
    part[2] = before_down(1, part[2])
    down_product(1, 1)
    middle[1] = before_weigh(1, middle[1])
    back[1] = send(weigh(1, 1).astype(BF), -1)
    finish(2)
    down_product(2, 0)
    part[3] = before_down(2, part[3])
    down_product(2, 1)
    finish(3)
    down_product(3, 0)
    forth[0] = send((weigh(3, 0) + middle[0].astype(F32)).astype(BF), 1)
    hidden[3, 1] = before_weigh(2, hidden[3, 1])
    term = [weigh(2, g) for g in range(2)]
    down_product(3, 1)
    back = before_weigh(3, back)
    theirs = send((term[1] + back[1].astype(F32)).astype(BF), flip=1)
    forth[1] = send((weigh(3, 1) + middle[1].astype(F32)).astype(BF), 1, 1)
    mine = (term[0] + back[0].astype(F32) + forth[0].astype(F32)).astype(BF)
    far = (theirs.astype(F32) + forth[1].astype(F32)).astype(BF)

    mixed = jnp.zeros(tokens.shape, BF)
    for r, piece in enumerate(
        [mine[:, :quarter], far[:, :quarter], mine[:, quarter:], far[:, quarter:]]
    ):
        mixed = lax.dynamic_update_slice_in_dim(mixed, piece, (d ^ r) * quarter, axis=1)
    return mixed


def solution(mesh):
    placed = (
        P(("dp", "expert"), None),
        P("expert", "dp", None),
        P("expert", None, "dp"),
        P(("dp", "expert"), None),
        P(("dp", "expert"), None),
    )
    short = mesh.shape["expert"] == 8 and mesh.shape["dp"] == 4
    return jax.shard_map(
        paired if short else gathered,
        mesh=mesh,
        in_specs=placed,
        out_specs=P(("dp", "expert"), None),
        check_vma=False,
    )
```

```python
import jax
import jax.numpy as jnp
from jax import lax
from jax.sharding import PartitionSpec as P

BF = jnp.bfloat16
F32 = jnp.float32

def gathered(tokens, gate_up, down_proj, expert_ids, gate_weights):
    owners = lax.axis_size("expert")
    tok_rows = tokens.shape[0]
    width = tokens.shape[1]
    hidden_units = down_proj.shape[1]
    slots = 4 * tok_rows // owners
    total_rows = owners * slots
    owner_ids = jnp.arange(owners, dtype=jnp.int32)
    matches = expert_ids[:, :, None] == owner_ids[None, None, :]
    hits = jnp.sum(matches.astype(jnp.int32), axis=1)
    pick_weight = jnp.sum(
        jnp.where(matches, gate_weights[:, :, None].astype(F32), 0.0), axis=1
    )
    before = jnp.cumsum(hits, axis=0) - hits
    target = jnp.where(hits > 0, owner_ids[None, :] * slots + before, -1)
    slot_owner = jnp.arange(total_rows, dtype=jnp.int32) // slots
    slot_ids = jnp.arange(total_rows, dtype=jnp.int32)
    placed = jnp.take(target, slot_owner, axis=1) == slot_ids[None, :]
    place_bf = placed.astype(BF)
    outgoing = jnp.dot(place_bf.T, tokens, preferred_element_type=F32).astype(BF)
    arrived = lax.all_to_all(
        outgoing.reshape(owners, slots, width), "expert", split_axis=0, concat_axis=0, tiled=True
    )
    rows = arrived.reshape(total_rows, width)
    gu = jnp.dot(
        rows,
        lax.all_gather(gate_up, "dp", axis=1, tiled=True)[0],
        preferred_element_type=F32,
    )
    hidden = (jax.nn.silu(gu[:, :hidden_units]) * gu[:, hidden_units:]).astype(BF)
    result = jnp.dot(
        hidden,
        lax.all_gather(down_proj, "dp", axis=2, tiled=True)[0],
        preferred_element_type=F32,
    ).astype(BF)
    returned = lax.all_to_all(
        result.reshape(owners, slots, width), "expert", split_axis=0, concat_axis=0, tiled=True
    )
    weighted = (place_bf.astype(F32) * jnp.take(pick_weight, slot_owner, axis=1)).astype(BF)
    mixed = jnp.dot(weighted, returned.reshape(total_rows, width), preferred_element_type=F32)
    return mixed.astype(BF)


def paired(tokens, gate_up, down_proj, expert_ids, gate_weights):
    owners = lax.axis_size("expert")
    chips = owners // 2
    tok = tokens.shape[0]
    quarter = gate_up.shape[1]
    half = 2 * quarter
    ff = down_proj.shape[1]
    slots = 4 * tok // owners
    chunk = 2 * slots
    d = lax.axis_index("dp")
    e = lax.axis_index("expert")
    gate, down = gate_up[0], down_proj[0]
    together = lax.optimization_barrier

    def send(value, along=0, flip=0, core=0):
        return lax.ppermute(
            value,
            ("dp", "expert"),
            [
                (i * owners + j, (i ^ flip) * owners + ((j ^ core) + 2 * along) % owners)
                for i in range(4)
                for j in range(owners)
            ],
        )

    def depths(r):
        return lax.dynamic_slice_in_dim(tokens, (d ^ r) * quarter, quarter, axis=1)

    info = jnp.concatenate([expert_ids.T.astype(BF), gate_weights.T], axis=1)
    info = jnp.pad(info, ((0, 0), (0, half - 2 * tok)))

    def payload(r):
        return jnp.concatenate([jnp.concatenate([depths(r), depths(r + 1)], axis=1), info])

    first, second = payload(0), payload(2)
    gate_x = send(gate, flip=1)

    seen = [{0: first, 1: send(first, 1)}, {0: send(second, flip=2)}]
    seen[0][0], seen[1][0], down = together((seen[0][0], seen[1][0], down))
    down_y = send(down, flip=2)
    seen[1][1] = send(seen[1][0], 1)
    for held in seen:
        held[3] = send(held[0], -1)
        held[2] = send(held[1], 1)
    downs = jnp.concatenate([down, down_y], axis=1)
    seen[1][2], downs = together((seen[1][2], downs))

    chosen = jnp.stack([e, e ^ 1]).astype(jnp.int32)
    earlier = jnp.triu(jnp.ones((tok, tok), BF), 1)

    def places(info):
        matches = info[:, None, :, :tok].astype(jnp.int32) == chosen[:, None, None]
        hits = jnp.any(matches, axis=2)
        weight = jnp.sum(jnp.where(matches, info[:, None, :, tok:].astype(F32), 0.0), axis=2)
        rank = jnp.dot(hits.astype(BF), earlier, preferred_element_type=F32)
        rank = jnp.where(hits, rank, -1.0)
        place = (rank[..., None, :] == jnp.arange(slots, dtype=F32)[:, None]).astype(BF)
        pay = place * weight[..., None, :].astype(BF)
        return place, pay.reshape(chips, chunk, tok)

    infos = [jnp.stack([seen[g][k][tok:, : 2 * tok] for k in range(chips)]) for g in range(2)]
    helds = [jnp.stack([seen[g][k][:tok] for k in range(chips)]) for g in range(2)]
    info_x = send(infos[0], flip=1)
    place0, pay0 = places(infos[0])
    place1, _ = places(infos[1])

    def choose(place, held):
        def of(expert):
            return jnp.einsum(
                "zst,ztk->zsk", place[:, expert], held, preferred_element_type=F32
            ).astype(BF)

        other = send(of(1), core=1)
        return jnp.concatenate([of(0), other], axis=1)

    chosen0, chosen1 = choose(place0, helds[0]), choose(place1, helds[1])

    chosen1, gate_x = together((chosen1, gate_x))
    weights = jnp.concatenate([gate, gate_x])

    def product(rows, lo=0, hi=2 * ff):
        flat = rows.reshape(-1, half)
        return jnp.dot(flat, weights[:, lo:hi], preferred_element_type=F32).reshape(
            chips, chunk, hi - lo
        )

    order = (2, 1, 0, 3)
    gates = product(chosen1, 0, ff).astype(BF)
    gates, chosen1 = together((gates, chosen1))
    gate_part = send(gates[order[0]], flip=2)
    ups = product(chosen1, ff).astype(BF)
    ups, chosen0 = together((ups, chosen0))
    part = [send(ups[order[0]], flip=2)]
    chosen0, gate_part, gates, ups = together((chosen0, gate_part, gates, ups))
    part[0] = jnp.concatenate([gate_part, part[0]], axis=1)

    def whole(q):
        return jnp.concatenate([gates[order[q]], ups[order[q]]], axis=1)

    second = whole(1)
    chosen0, second = together((chosen0, second))
    part.append(send(second, flip=2))
    near = product(chosen0)
    pays = [pay0]

    hidden, out, came = {}, {}, {}

    def finish(q):
        gu = near[order[q]] + part[q].astype(F32)
        own = (jax.nn.silu(gu[:, :ff]) * gu[:, ff:]).astype(BF)
        hidden[q, 0], hidden[q, 1] = own, send(own, flip=1)

    def down_product(q, g):
        value = jnp.dot(hidden[q, g], downs, preferred_element_type=F32).astype(BF)
        value = value.reshape(2, slots, half)
        out[q, g], came[q, g] = value[0], send(value[1], core=1)

    def weigh(q, g):
        rows = jnp.concatenate([out[q, g], came[q, g]])
        return lax.dot_general(
            pays[g][order[q]], rows, (((0,), (0,)), ((), ())), preferred_element_type=F32
        )

    def before_weigh(q, value):
        came[q, 1], value = together((came[q, 1], value))
        return value

    def before_down(q, value):
        hidden[q, 1], value = together((hidden[q, 1], value))
        return value

    middle, back, forth = {}, {}, {}
    finish(0)
    hidden[0, 0], info_x = together((hidden[0, 0], info_x))
    down_product(0, 0)
    pays.append(places(info_x)[1])
    middle[0] = weigh(0, 0).astype(BF)
    middle[0], gates, ups = together((middle[0], gates, ups))
    part += [send(whole(q), flip=2) for q in range(2, chips)]
    middle[0] = send(middle[0], 1)
    down_product(0, 1)
    middle[0], part[1] = before_weigh(0, (middle[0], part[1]))
    middle[1] = send(weigh(0, 1).astype(BF), 1)
    finish(1)
    down_product(1, 0)
    back[0] = send(weigh(1, 0).astype(BF), -1)
    part[2] = before_down(1, part[2])
    down_product(1, 1)
    middle[1] = before_weigh(1, middle[1])
    back[1] = send(weigh(1, 1).astype(BF), -1)
    finish(2)
    down_product(2, 0)
    part[3] = before_down(2, part[3])
    down_product(2, 1)
    finish(3)
    down_product(3, 0)
    forth[0] = send((weigh(3, 0) + middle[0].astype(F32)).astype(BF), 1)
    hidden[3, 1] = before_weigh(2, hidden[3, 1])
    term = [weigh(2, g) for g in range(2)]
    down_product(3, 1)
    back = before_weigh(3, back)
    theirs = send((term[1] + back[1].astype(F32)).astype(BF), flip=1)
    forth[1] = send((weigh(3, 1) + middle[1].astype(F32)).astype(BF), 1, 1)
    mine = (term[0] + back[0].astype(F32) + forth[0].astype(F32)).astype(BF)
    far = (theirs.astype(F32) + forth[1].astype(F32)).astype(BF)

    mixed = jnp.zeros(tokens.shape, BF)
    for r, piece in enumerate(
        [mine[:, :quarter], far[:, :quarter], mine[:, quarter:], far[:, quarter:]]
    ):
        mixed = lax.dynamic_update_slice_in_dim(mixed, piece, (d ^ r) * quarter, axis=1)
    return mixed


def solution(mesh):
    placed = (
        P(("dp", "expert"), None),
        P("expert", "dp", None),
        P("expert", None, "dp"),
        P(("dp", "expert"), None),
        P(("dp", "expert"), None),
    )
    short = mesh.shape["expert"] == 8 and mesh.shape["dp"] == 4
    return jax.shard_map(
        paired if short else gathered,
        mesh=mesh,
        in_specs=placed,
        out_specs=P(("dp", "expert"), None),
        check_vma=False,
    )
```

```python
import jax
import jax.numpy as jnp
from jax import lax
from jax.sharding import PartitionSpec as P

BF = jnp.bfloat16
F32 = jnp.float32

def gathered(tokens, gate_up, down_proj, expert_ids, gate_weights):
    owners = lax.axis_size("expert")
    tok_rows = tokens.shape[0]
    width = tokens.shape[1]
    hidden_units = down_proj.shape[1]
    slots = 4 * tok_rows // owners
    total_rows = owners * slots
    owner_ids = jnp.arange(owners, dtype=jnp.int32)
    matches = expert_ids[:, :, None] == owner_ids[None, None, :]
    hits = jnp.sum(matches.astype(jnp.int32), axis=1)
    pick_weight = jnp.sum(
        jnp.where(matches, gate_weights[:, :, None].astype(F32), 0.0), axis=1
    )
    before = jnp.cumsum(hits, axis=0) - hits
    target = jnp.where(hits > 0, owner_ids[None, :] * slots + before, -1)
    slot_owner = jnp.arange(total_rows, dtype=jnp.int32) // slots
    slot_ids = jnp.arange(total_rows, dtype=jnp.int32)
    placed = jnp.take(target, slot_owner, axis=1) == slot_ids[None, :]
    place_bf = placed.astype(BF)
    outgoing = jnp.dot(place_bf.T, tokens, preferred_element_type=F32).astype(BF)
    arrived = lax.all_to_all(
        outgoing.reshape(owners, slots, width), "expert", split_axis=0, concat_axis=0, tiled=True
    )
    rows = arrived.reshape(total_rows, width)
    gu = jnp.dot(
        rows,
        lax.all_gather(gate_up, "dp", axis=1, tiled=True)[0],
        preferred_element_type=F32,
    )
    hidden = (jax.nn.silu(gu[:, :hidden_units]) * gu[:, hidden_units:]).astype(BF)
    result = jnp.dot(
        hidden,
        lax.all_gather(down_proj, "dp", axis=2, tiled=True)[0],
        preferred_element_type=F32,
    ).astype(BF)
    returned = lax.all_to_all(
        result.reshape(owners, slots, width), "expert", split_axis=0, concat_axis=0, tiled=True
    )
    weighted = (place_bf.astype(F32) * jnp.take(pick_weight, slot_owner, axis=1)).astype(BF)
    mixed = jnp.dot(weighted, returned.reshape(total_rows, width), preferred_element_type=F32)
    return mixed.astype(BF)


def paired(tokens, gate_up, down_proj, expert_ids, gate_weights):
    owners = lax.axis_size("expert")
    chips = owners // 2
    tok = tokens.shape[0]
    quarter = gate_up.shape[1]
    half = 2 * quarter
    ff = down_proj.shape[1]
    slots = 4 * tok // owners
    chunk = 2 * slots
    d = lax.axis_index("dp")
    e = lax.axis_index("expert")
    gate, down = gate_up[0], down_proj[0]
    together = lax.optimization_barrier

    def send(value, along=0, flip=0, core=0):
        return lax.ppermute(
            value,
            ("dp", "expert"),
            [
                (i * owners + j, (i ^ flip) * owners + ((j ^ core) + 2 * along) % owners)
                for i in range(4)
                for j in range(owners)
            ],
        )

    def depths(r):
        return lax.dynamic_slice_in_dim(tokens, (d ^ r) * quarter, quarter, axis=1)

    info = jnp.concatenate([expert_ids.T.astype(BF), gate_weights.T], axis=1)
    info = jnp.pad(info, ((0, 0), (0, half - 2 * tok)))

    def payload(r):
        return jnp.concatenate([jnp.concatenate([depths(r), depths(r + 1)], axis=1), info])

    first, second = payload(0), payload(2)
    gate_x = send(gate, flip=1)

    seen = [{0: first, 1: send(first, 1)}, {0: send(second, flip=2)}]
    seen[0][0], seen[1][0], down = together((seen[0][0], seen[1][0], down))
    down_y = send(down, flip=2)
    seen[1][1] = send(seen[1][0], 1)
    for held in seen:
        held[3] = send(held[0], -1)
        held[2] = send(held[1], 1)
    downs = jnp.concatenate([down, down_y], axis=1)
    seen[1][2], downs = together((seen[1][2], downs))

    chosen = jnp.stack([e, e ^ 1]).astype(jnp.int32)
    earlier = jnp.triu(jnp.ones((tok, tok), BF), 1)

    def places(info):
        matches = info[:, None, :, :tok].astype(jnp.int32) == chosen[:, None, None]
        hits = jnp.any(matches, axis=2)
        weight = jnp.sum(jnp.where(matches, info[:, None, :, tok:].astype(F32), 0.0), axis=2)
        rank = jnp.dot(hits.astype(BF), earlier, preferred_element_type=F32)
        rank = jnp.where(hits, rank, -1.0)
        place = (rank[..., None, :] == jnp.arange(slots, dtype=F32)[:, None]).astype(BF)
        pay = place * weight[..., None, :].astype(BF)
        return place, pay.reshape(chips, chunk, tok)

    infos = [jnp.stack([seen[g][k][tok:, : 2 * tok] for k in range(chips)]) for g in range(2)]
    helds = [jnp.stack([seen[g][k][:tok] for k in range(chips)]) for g in range(2)]
    info_x = send(infos[0], flip=1)
    place0, pay0 = places(infos[0])
    place1, _ = places(infos[1])

    def choose(place, held):
        def of(expert):
            return jnp.einsum(
                "zst,ztk->zsk", place[:, expert], held, preferred_element_type=F32
            ).astype(BF)

        other = send(of(1), core=1)
        return jnp.concatenate([of(0), other], axis=1)

    chosen0, chosen1 = choose(place0, helds[0]), choose(place1, helds[1])

    chosen1, gate_x = together((chosen1, gate_x))
    weights = jnp.concatenate([gate, gate_x])

    def product(rows, lo=0, hi=2 * ff):
        flat = rows.reshape(-1, half)
        return jnp.dot(flat, weights[:, lo:hi], preferred_element_type=F32).reshape(
            chips, chunk, hi - lo
        )

    order = (2, 1, 0, 3)
    gates = product(chosen1, 0, ff).astype(BF)
    gates, chosen1 = together((gates, chosen1))
    gate_part = send(gates[order[0]], flip=2)
    ups = product(chosen1, ff).astype(BF)
    ups, chosen0 = together((ups, chosen0))
    part = [send(ups[order[0]], flip=2)]
    chosen0, gate_part, gates, ups = together((chosen0, gate_part, gates, ups))
    part[0] = jnp.concatenate([gate_part, part[0]], axis=1)

    def whole(q):
        return jnp.concatenate([gates[order[q]], ups[order[q]]], axis=1)

    second = whole(1)
    chosen0, second = together((chosen0, second))
    part.append(send(second, flip=2))
    near = product(chosen0)
    pays = [pay0]

    hidden, out, came = {}, {}, {}

    def finish(q):
        gu = near[order[q]] + part[q].astype(F32)
        own = (jax.nn.silu(gu[:, :ff]) * gu[:, ff:]).astype(BF)
        hidden[q, 0] = own
        if q > 0:
            hidden[q, 1] = send(own, flip=1)

    def down_product(q, g):
        value = jnp.dot(hidden[q, g], downs, preferred_element_type=F32).astype(BF)
        value = value.reshape(2, slots, half)
        out[q, g], came[q, g] = value[0], send(value[1], core=1)

    def weigh(q, g):
        rows = jnp.concatenate([out[q, g], came[q, g]])
        return lax.dot_general(
            pays[g][order[q]], rows, (((0,), (0,)), ((), ())), preferred_element_type=F32
        )

    def before_weigh(q, value):
        came[q, 1], value = together((came[q, 1], value))
        return value

    def before_down(q, value):
        hidden[q, 1], value = together((hidden[q, 1], value))
        return value

    middle, back, forth = {}, {}, {}
    finish(0)
    hidden[0, 0], info_x = together((hidden[0, 0], info_x))
    down_product(0, 0)
    out[0, 0], own = together((out[0, 0], hidden[0, 0]))
    hidden[0, 1] = send(own, flip=1)
    pays.append(places(info_x)[1])
    middle[0] = weigh(0, 0).astype(BF)
    middle[0], gates, ups = together((middle[0], gates, ups))
    part += [send(whole(q), flip=2) for q in range(2, chips)]
    middle[0] = send(middle[0], 1)
    down_product(0, 1)
    middle[0], part[1] = before_weigh(0, (middle[0], part[1]))
    middle[1] = send(weigh(0, 1).astype(BF), 1)
    finish(1)
    down_product(1, 0)
    back[0] = send(weigh(1, 0).astype(BF), -1)
    part[2] = before_down(1, part[2])
    down_product(1, 1)
    middle[1] = before_weigh(1, middle[1])
    back[1] = send(weigh(1, 1).astype(BF), -1)
    finish(2)
    down_product(2, 0)
    part[3] = before_down(2, part[3])
    down_product(2, 1)
    finish(3)
    down_product(3, 0)
    forth[0] = send((weigh(3, 0) + middle[0].astype(F32)).astype(BF), 1)
    hidden[3, 1] = before_weigh(2, hidden[3, 1])
    term = [weigh(2, g) for g in range(2)]
    down_product(3, 1)
    back = before_weigh(3, back)
    theirs = send((term[1] + back[1].astype(F32)).astype(BF), flip=1)
    forth[1] = send((weigh(3, 1) + middle[1].astype(F32)).astype(BF), 1, 1)
    mine = (term[0] + back[0].astype(F32) + forth[0].astype(F32)).astype(BF)
    far = (theirs.astype(F32) + forth[1].astype(F32)).astype(BF)

    mixed = jnp.zeros(tokens.shape, BF)
    for r, piece in enumerate(
        [mine[:, :quarter], far[:, :quarter], mine[:, quarter:], far[:, quarter:]]
    ):
        mixed = lax.dynamic_update_slice_in_dim(mixed, piece, (d ^ r) * quarter, axis=1)
    return mixed


def solution(mesh):
    placed = (
        P(("dp", "expert"), None),
        P("expert", "dp", None),
        P("expert", None, "dp"),
        P(("dp", "expert"), None),
        P(("dp", "expert"), None),
    )
    short = mesh.shape["expert"] == 8 and mesh.shape["dp"] == 4
    return jax.shard_map(
        paired if short else gathered,
        mesh=mesh,
        in_specs=placed,
        out_specs=P(("dp", "expert"), None),
        check_vma=False,
    )
```

```python
import jax
import jax.numpy as jnp
from jax import lax
from jax.sharding import PartitionSpec as P

BF = jnp.bfloat16
F32 = jnp.float32

def gathered(tokens, gate_up, down_proj, expert_ids, gate_weights):
    owners = lax.axis_size("expert")
    tok_rows = tokens.shape[0]
    width = tokens.shape[1]
    hidden_units = down_proj.shape[1]
    slots = 4 * tok_rows // owners
    total_rows = owners * slots
    owner_ids = jnp.arange(owners, dtype=jnp.int32)
    matches = expert_ids[:, :, None] == owner_ids[None, None, :]
    hits = jnp.sum(matches.astype(jnp.int32), axis=1)
    pick_weight = jnp.sum(
        jnp.where(matches, gate_weights[:, :, None].astype(F32), 0.0), axis=1
    )
    before = jnp.cumsum(hits, axis=0) - hits
    target = jnp.where(hits > 0, owner_ids[None, :] * slots + before, -1)
    slot_owner = jnp.arange(total_rows, dtype=jnp.int32) // slots
    slot_ids = jnp.arange(total_rows, dtype=jnp.int32)
    placed = jnp.take(target, slot_owner, axis=1) == slot_ids[None, :]
    place_bf = placed.astype(BF)
    outgoing = jnp.dot(place_bf.T, tokens, preferred_element_type=F32).astype(BF)
    arrived = lax.all_to_all(
        outgoing.reshape(owners, slots, width), "expert", split_axis=0, concat_axis=0, tiled=True
    )
    rows = arrived.reshape(total_rows, width)
    gu = jnp.dot(
        rows,
        lax.all_gather(gate_up, "dp", axis=1, tiled=True)[0],
        preferred_element_type=F32,
    )
    hidden = (jax.nn.silu(gu[:, :hidden_units]) * gu[:, hidden_units:]).astype(BF)
    result = jnp.dot(
        hidden,
        lax.all_gather(down_proj, "dp", axis=2, tiled=True)[0],
        preferred_element_type=F32,
    ).astype(BF)
    returned = lax.all_to_all(
        result.reshape(owners, slots, width), "expert", split_axis=0, concat_axis=0, tiled=True
    )
    weighted = (place_bf.astype(F32) * jnp.take(pick_weight, slot_owner, axis=1)).astype(BF)
    mixed = jnp.dot(weighted, returned.reshape(total_rows, width), preferred_element_type=F32)
    return mixed.astype(BF)


def paired(tokens, gate_up, down_proj, expert_ids, gate_weights):
    owners = lax.axis_size("expert")
    chips = owners // 2
    tok = tokens.shape[0]
    quarter = gate_up.shape[1]
    half = 2 * quarter
    ff = down_proj.shape[1]
    slots = 4 * tok // owners
    chunk = 2 * slots
    d = lax.axis_index("dp")
    e = lax.axis_index("expert")
    gate, down = gate_up[0], down_proj[0]
    together = lax.optimization_barrier

    def send(value, along=0, flip=0, core=0):
        return lax.ppermute(
            value,
            ("dp", "expert"),
            [
                (i * owners + j, (i ^ flip) * owners + ((j ^ core) + 2 * along) % owners)
                for i in range(4)
                for j in range(owners)
            ],
        )

    def depths(r):
        return lax.dynamic_slice_in_dim(tokens, (d ^ r) * quarter, quarter, axis=1)

    info = jnp.concatenate([expert_ids.T.astype(BF), gate_weights.T], axis=1)
    info = jnp.pad(info, ((0, 0), (0, half - 2 * tok)))

    def payload(r):
        return jnp.concatenate([jnp.concatenate([depths(r), depths(r + 1)], axis=1), info])

    first, second = payload(0), payload(2)
    gate_x = send(gate, flip=1)

    seen = [{0: first, 1: send(first, 1)}, {0: send(second, flip=2)}]
    seen[0][0], seen[1][0], down = together((seen[0][0], seen[1][0], down))
    down_y = send(down, flip=2)
    seen[1][1] = send(seen[1][0], 1)
    for held in seen:
        held[3] = send(held[0], -1)
        held[2] = send(held[1], 1)
    downs = jnp.concatenate([down, down_y], axis=1)
    seen[1][2], downs = together((seen[1][2], downs))

    chosen = jnp.stack([e, e ^ 1]).astype(jnp.int32)
    earlier = jnp.triu(jnp.ones((tok, tok), BF), 1)

    def places(info):
        matches = info[:, None, :, :tok].astype(jnp.int32) == chosen[:, None, None]
        hits = jnp.any(matches, axis=2)
        weight = jnp.sum(jnp.where(matches, info[:, None, :, tok:].astype(F32), 0.0), axis=2)
        rank = jnp.dot(hits.astype(BF), earlier, preferred_element_type=F32)
        rank = jnp.where(hits, rank, -1.0)
        place = (rank[..., None, :] == jnp.arange(slots, dtype=F32)[:, None]).astype(BF)
        pay = place * weight[..., None, :].astype(BF)
        return place, pay.reshape(chips, chunk, tok)

    infos = [jnp.stack([seen[g][k][tok:, : 2 * tok] for k in range(chips)]) for g in range(2)]
    helds = [jnp.stack([seen[g][k][:tok] for k in range(chips)]) for g in range(2)]
    info_x = send(infos[0], flip=1)
    place0, pay0 = places(infos[0])
    place1, _ = places(infos[1])

    def choose(place, held):
        def of(expert):
            return jnp.einsum(
                "zst,ztk->zsk", place[:, expert], held, preferred_element_type=F32
            ).astype(BF)

        other = send(of(1), core=1)
        return jnp.concatenate([of(0), other], axis=1)

    chosen0, chosen1 = choose(place0, helds[0]), choose(place1, helds[1])

    chosen1, gate_x = together((chosen1, gate_x))
    weights = jnp.concatenate([gate, gate_x])

    def product(rows, lo=0, hi=2 * ff):
        flat = rows.reshape(-1, half)
        return jnp.dot(flat, weights[:, lo:hi], preferred_element_type=F32).reshape(
            chips, chunk, hi - lo
        )

    order = (2, 1, 0, 3)
    gates = product(chosen1, 0, ff).astype(BF)
    gates, chosen1 = together((gates, chosen1))
    gate_part = send(gates[order[0]], flip=2)
    ups = product(chosen1, ff).astype(BF)
    ups, chosen0 = together((ups, chosen0))
    part = [send(ups[order[0]], flip=2)]
    chosen0, gate_part, gates, ups = together((chosen0, gate_part, gates, ups))
    part[0] = jnp.concatenate([gate_part, part[0]], axis=1)

    def whole(q):
        return jnp.concatenate([gates[order[q]], ups[order[q]]], axis=1)

    second = whole(1)
    chosen0, second = together((chosen0, second))
    part.append(send(second, flip=2))
    near = product(chosen0)
    pays = [pay0]

    hidden, out, came = {}, {}, {}

    def finish(q):
        gu = near[order[q]] + part[q].astype(F32)
        own = (jax.nn.silu(gu[:, :ff]) * gu[:, ff:]).astype(BF)
        hidden[q, 0], hidden[q, 1] = own, send(own, flip=1)

    def down_product(q, g):
        value = jnp.dot(hidden[q, g], downs, preferred_element_type=F32).astype(BF)
        value = value.reshape(2, slots, half)
        out[q, g], came[q, g] = value[0], send(value[1], core=1)

    def weigh(q, g):
        rows = jnp.concatenate([out[q, g], came[q, g]])
        return lax.dot_general(
            pays[g][order[q]], rows, (((0,), (0,)), ((), ())), preferred_element_type=F32
        )

    def before_weigh(q, value):
        came[q, 1], value = together((came[q, 1], value))
        return value

    def before_down(q, value):
        hidden[q, 1], value = together((hidden[q, 1], value))
        return value

    middle, back, forth = {}, {}, {}
    finish(0)
    hidden[0, 0], info_x = together((hidden[0, 0], info_x))
    down_product(0, 0)
    pays.append(places(info_x)[1])
    middle[0] = weigh(0, 0).astype(BF)
    middle[0], gates, ups = together((middle[0], gates, ups))
    part.append(send(whole(2), flip=2))
    middle[0] = send(middle[0], 1)
    down_product(0, 1)
    middle[0], part[1] = before_weigh(0, (middle[0], part[1]))
    middle[0], gates, ups = together((middle[0], gates, ups))
    part.append(send(whole(3), flip=2))
    middle[1] = send(weigh(0, 1).astype(BF), 1)
    finish(1)
    down_product(1, 0)
    back[0] = send(weigh(1, 0).astype(BF), -1)
    part[2] = before_down(1, part[2])
    down_product(1, 1)
    middle[1] = before_weigh(1, middle[1])
    back[1] = send(weigh(1, 1).astype(BF), -1)
    finish(2)
    down_product(2, 0)
    part[3] = before_down(2, part[3])
    down_product(2, 1)
    finish(3)
    down_product(3, 0)
    forth[0] = send((weigh(3, 0) + middle[0].astype(F32)).astype(BF), 1)
    hidden[3, 1] = before_weigh(2, hidden[3, 1])
    term = [weigh(2, g) for g in range(2)]
    down_product(3, 1)
    back = before_weigh(3, back)
    theirs = send((term[1] + back[1].astype(F32)).astype(BF), flip=1)
    forth[1] = send((weigh(3, 1) + middle[1].astype(F32)).astype(BF), 1, 1)
    mine = (term[0] + back[0].astype(F32) + forth[0].astype(F32)).astype(BF)
    far = (theirs.astype(F32) + forth[1].astype(F32)).astype(BF)

    mixed = jnp.zeros(tokens.shape, BF)
    for r, piece in enumerate(
        [mine[:, :quarter], far[:, :quarter], mine[:, quarter:], far[:, quarter:]]
    ):
        mixed = lax.dynamic_update_slice_in_dim(mixed, piece, (d ^ r) * quarter, axis=1)
    return mixed


def solution(mesh):
    placed = (
        P(("dp", "expert"), None),
        P("expert", "dp", None),
        P("expert", None, "dp"),
        P(("dp", "expert"), None),
        P(("dp", "expert"), None),
    )
    short = mesh.shape["expert"] == 8 and mesh.shape["dp"] == 4
    return jax.shard_map(
        paired if short else gathered,
        mesh=mesh,
        in_specs=placed,
        out_specs=P(("dp", "expert"), None),
        check_vma=False,
    )
```
